256 devices in a mesh: tm: 8 (over z), gx: 8 (over x, core), gy: 4 (over y).
Axes of the slice: x: 4, y: 4, z: 8, core: 2. Of those that a mesh axis runs over, the one named last changes fastest.
Arguments:
- state_starts: float32 [8, 64, 256, 512], P('tm', None, 'gx', 'gy'), may hold values from -4 to 4, as said below
- diffusivity: float32 [64], replicated, may hold values from 0.3 to 1.2
- wind: float32 [2, 64], replicated, may hold values from -0.6 to 0.6
Outputs:
- segment_ends: float32 [8, 64, 256, 512], P('tm', None, 'gx', 'gy')
The draws below stay inside these ranges and needn't reach their ends.
Inputs may be any that keep to these rules, and one draw needn't show every extreme that they name: `state_starts`: states of order one.
All inputs are finite; a program needn't handle non-finite values.
Results may differ from the reference program's by a relative error of at most 0.0001.
Values sent between devices are 32-bit elements; how exact they have to be, the bound alone decides.
No kernel may reach another device: no remote copies, remote signals or barrier semaphores. Data moves between devices by JAX's collectives and lax.ppermute only.
A program may use at most 64 MiB of HBM per device.

```python
import math
import jax
import jax.numpy as jnp

L = 64
SUB = 4
SEGMENTS = 8
NX = 256
NY = 512


def draw_state_starts(key, part):
    shape = (SEGMENTS, L, NX, NY)
    return jnp.clip(jax.random.normal(key, shape, jnp.float32), -4.0, 4.0)


def setup_inputs(seed: int = 0) -> dict:
    arg_keys = jax.random.split(jax.random.key(seed), 4)
    return {
        "state_starts": draw_state_starts(jax.random.fold_in(arg_keys[3], 71), 0),
        "diffusivity": jnp.clip(jnp.exp(jax.random.uniform(arg_keys[1], (L,), jnp.float32, math.log(0.3), math.log(1.2))), 0.3, 1.2),
        "wind": jnp.clip(jax.random.uniform(arg_keys[2], (2, L), jnp.float32, -0.6, 0.6), -0.6, 0.6),
    }


time_step = 0.2
weights_low = (0.375, 0.125, 0.0, 0.0)
weights_mid = (0.625, 0.875, 0.875, 0.625)
weights_high = (0.0, 0.0, 0.125, 0.375)


def advance(padded, diffuse, wind_east, wind_north, factor):
    centre = padded[:, 1:-1, 1:-1]
    east = padded[:, 2:, 1:-1]
    west = padded[:, :-2, 1:-1]
    north = padded[:, 1:-1, 2:]
    south = padded[:, 1:-1, :-2]
    laplace = east + west + north + south - 4.0 * centre
    slope = wind_east * (east - west) * 0.5 + wind_north * (north - south) * 0.5
    return centre + time_step * (factor * diffuse * laplace - centre * slope)


def pad_zero(field):
    return jnp.pad(field, ((0, 0), (1, 1), (1, 1)))


def restrict(field):
    levels, rows, cols = field.shape
    return field.reshape(levels, rows // 4, 4, cols // 4, 4).mean(axis=(2, 4))


def prolong(padded):
    levels, rows_ext, cols_ext = padded.shape
    coarse_rows = rows_ext - 2
    coarse_cols = cols_ext - 2
    parts = [weights_low[offset] * padded[:, :-2, :] + weights_mid[offset] * padded[:, 1:-1, :] + weights_high[offset] * padded[:, 2:, :] for offset in range(4)]
    along = jnp.stack(parts, axis=2).reshape(levels, 4 * coarse_rows, cols_ext)
    parts = [weights_low[offset] * along[:, :, :-2] + weights_mid[offset] * along[:, :, 1:-1] + weights_high[offset] * along[:, :, 2:] for offset in range(4)]
    return jnp.stack(parts, axis=3).reshape(levels, 4 * coarse_rows, 4 * coarse_cols)


def reference(state_starts, diffusivity, wind):
    diffuse = diffusivity[:, None, None]
    wind_east = wind[0][:, None, None]
    wind_north = wind[1][:, None, None]
    fine_ends = []
    old_images = []
    coarse_first = restrict(state_starts[0])
    for segment in range(SEGMENTS):
        field = state_starts[segment]
        for substep in range(SUB):
            field = advance(pad_zero(field), diffuse, wind_east, wind_north, 1.0)
        fine_ends.append(field)
        coarse_old = restrict(state_starts[segment])
        old_images.append(advance(pad_zero(coarse_old), diffuse, wind_east, wind_north, 0.25))
    coarse = coarse_first
    results = []
    for segment in range(SEGMENTS):
        change = advance(pad_zero(coarse), diffuse, wind_east, wind_north, 0.25) - old_images[segment]
        ending = fine_ends[segment] + prolong(pad_zero(change))
        results.append(ending)
        coarse = restrict(ending)
    return jnp.stack(results)
```

```python
import jax
import jax.numpy as jnp
from jax import lax
from jax.experimental import pallas as pl
from jax.experimental.pallas import tpu as pltpu
from jax.sharding import PartitionSpec as P

SUB = 4
STEP = 0.2
LEVELS = 64
NX = 32
HALF = 64
CX = NX // 4
CY = HALF // 4
W = 128
WEIGHTS_LOW = (0.375, 0.125, 0.0, 0.0)
WEIGHTS_MID = (0.625, 0.875, 0.875, 0.625)
WEIGHTS_HIGH = (0.0, 0.0, 0.125, 0.375)
BLEND = (0.125, 0.75, 0.125)
F32 = jnp.float32

STRIP = 4 * HALF + CY
SIDE = 20 * 8 + 8
FROWS = 88
CROWS = 40
OROWS = 24


def lanes(rows):
    return lax.broadcasted_iota(jnp.int32, (rows, W), 1)


def rows_of(rows):
    return lax.broadcasted_iota(jnp.int32, (rows, W), 0)


def low(rows):
    return lanes(rows) < LEVELS


def swap(value):
    return pltpu.roll(value, LEVELS, 1)


def coarse_rows(ref, start, count):
    total = ref[pl.ds(start, count, stride=4), :]
    for offset in range(1, 4):
        total = total + ref[pl.ds(start + offset, count, stride=4), :]
    return total * (1.0 / 16.0)


def pack_kernel(u_ref, t_ref, first_ref, last_ref, sum_ref):
    lo = low(HALF)
    for x in range(0, NX, 2):
        both = jnp.concatenate(
            [u_ref[pl.ds(x, LEVELS, stride=NX), :], u_ref[pl.ds(x + 1, LEVELS, stride=NX), :]], axis=0
        ).T
        top = both[:HALF]
        bottom = both[HALF:]
        t_ref[x * HALF : (x + 1) * HALF, :] = jnp.where(lo, top, swap(bottom))
        t_ref[(x + 1) * HALF : (x + 2) * HALF, :] = jnp.where(lo, swap(top), bottom)

    def row(x):
        return t_ref[x * HALF : (x + 1) * HALF, :]

    first_ref[: 4 * HALF, :] = t_ref[: 4 * HALF, :]
    sum_ref[...] = (row(4) + row(5)) + (row(6) + row(7))
    first_ref[4 * HALF :, :] = coarse_rows(sum_ref, 0, CY)
    last_ref[: 4 * HALF, :] = t_ref[(NX - 4) * HALF :, :]
    sum_ref[...] = (row(NX - 8) + row(NX - 7)) + (row(NX - 6) + row(NX - 5))
    last_ref[4 * HALF :, :] = coarse_rows(sum_ref, 0, CY)


def side_kernel(t_ref, west_ref, east_ref, left_ref, right_ref):
    lo = low(8)

    def edge(x, start):
        if x < 0:
            base = (x + 4) * HALF
            return west_ref[base + start : base + start + 8, :]
        if x >= NX:
            base = (x - NX) * HALF
            return east_ref[base + start : base + start + 8, :]
        return t_ref[x * HALF + start : x * HALF + start + 8, :]

    for i in range(20):
        left_ref[8 * i : 8 * i + 8, :] = jnp.where(lo, edge(i - 4, 0), swap(edge(i + 16, 0)))
        right_ref[8 * i : 8 * i + 8, :] = jnp.where(
            lo, swap(edge(i - 4, HALF - 8)), edge(i + 16, HALF - 8)
        )
    base = 4 * HALF
    left_ref[160:168, :] = jnp.where(lo, west_ref[base : base + 8, :], swap(east_ref[base : base + 8, :]))
    right_ref[160:168, :] = jnp.where(
        lo, swap(west_ref[base + 8 : base + 16, :]), east_ref[base + 8 : base + 16, :]
    )


def both_halves(values):
    return jnp.concatenate([values, values], axis=1)


def fine_kernel(
    place_ref, t_ref, west_ref, east_ref, left_ref, right_ref, diffuse_ref, wind_ref,
    end_ref, image_ref, send_ref,
    a_ref, b_ref, sum_ref, coarse_ref, change_ref, blend_ref, part_ref,
):
    first_segment = place_ref[0] == 0
    at_west = place_ref[1] == 0
    at_east = place_ref[1] == 7
    at_left = place_ref[2] == 0
    at_right = place_ref[2] == 3
    lo8 = low(8)
    zero8 = jnp.zeros((8, W), F32)

    for i in range(40):
        x = i - 4
        if x < 0:
            source, base, outside = west_ref, (x + 4) * HALF, at_west
        elif x >= NX:
            source, base, outside = east_ref, (x - NX) * HALF, at_east
        else:
            source, base, outside = t_ref, x * HALF, None
        rows = source[base : base + HALF, :]
        j = i % 20
        from_left = left_ref[8 * j : 8 * j + 8, :]
        from_right = right_ref[8 * j : 8 * j + 8, :]
        if i >= 20:
            from_left = swap(from_left)
        else:
            from_right = swap(from_right)
        from_left = jnp.where(at_left, zero8, from_left)
        from_right = jnp.where(at_right, zero8, from_right)
        before = jnp.where(lo8, from_left, swap(rows[HALF - 8 :]))
        after = jnp.where(lo8, swap(rows[:8]), from_right)
        if outside is not None:
            rows = jnp.where(outside, jnp.zeros_like(rows), rows)
            before = jnp.where(outside, zero8, before)
            after = jnp.where(outside, zero8, after)
        start = i * FROWS
        a_ref[start : start + 4, :] = zero8[:4]
        a_ref[start + 4 : start + 12, :] = before
        a_ref[start + 12 : start + 76, :] = rows
        a_ref[start + 76 : start + 84, :] = after
        a_ref[start + 84 : start + 88, :] = zero8[:4]

    diffuse = both_halves(diffuse_ref[...])
    wind = both_halves(wind_ref[...])
    spread = jnp.broadcast_to(STEP * diffuse, (8, W))
    along_x = jnp.broadcast_to((0.5 * STEP) * wind[0:1], (8, W))
    along_y = jnp.broadcast_to((0.5 * STEP) * wind[1:2], (8, W))

    def advanced(centre, east, west, north, south, kd):
        slope = along_x * (east - west) + along_y * (north - south)
        return centre + (kd * ((east + west) + (north + south) - 4.0 * centre) - centre * slope)

    coarse_ref[...] = jnp.zeros_like(coarse_ref)
    for j in range(10):
        base = 4 * j * FROWS
        sum_ref[...] = (a_ref[base : base + FROWS, :] + a_ref[base + FROWS : base + 2 * FROWS, :]) + (
            a_ref[base + 2 * FROWS : base + 3 * FROWS, :] + a_ref[base + 3 * FROWS : base + 4 * FROWS, :]
        )
        start = (j + 1) * CROWS
        coarse_ref[start + 7 : start + 27, :] = coarse_rows(sum_ref, 4, 20)
    left_corner = left_ref[160:168, :]
    right_corner = right_ref[160:168, :]
    for source, start, outside, is_west in (
        (west_ref, 0, at_west, True),
        (east_ref, 11 * CROWS, at_east, False),
    ):
        rows = source[4 * HALF :, :]
        from_left = left_corner if is_west else swap(left_corner)
        from_right = swap(right_corner) if is_west else right_corner
        from_left = jnp.where(at_left, zero8, from_left)
        from_right = jnp.where(at_right, zero8, from_right)
        before = jnp.where(lo8, from_left, swap(rows[8:]))
        after = jnp.where(lo8, swap(rows[:8]), from_right)
        coarse_ref[start + 1 : start + 9, :] = jnp.where(outside, zero8, before)
        coarse_ref[start + 9 : start + 25, :] = jnp.where(outside, jnp.zeros_like(rows), rows)
        coarse_ref[start + 25 : start + 33, :] = jnp.where(outside, zero8, after)

    for j in range(10):
        for tile in range(3):
            r = (j + 1) * CROWS + 8 + 8 * tile
            image = advanced(
                coarse_ref[r : r + 8, :],
                coarse_ref[r + CROWS : r + CROWS + 8, :],
                coarse_ref[r - CROWS : r - CROWS + 8, :],
                coarse_ref[r + 1 : r + 9, :],
                coarse_ref[r - 1 : r + 7, :],
                0.25 * spread,
            )
            cy = rows_of(8) + (8 * tile - 1)
            outside = cy > CY
            if tile == 0:
                outside = jnp.logical_or(outside, jnp.logical_and(at_left, jnp.logical_and(cy < 0, lo8)))
            if tile == 2:
                outside = jnp.logical_or(
                    outside, jnp.logical_and(at_right, jnp.logical_and(cy >= CY, jnp.logical_not(lo8)))
                )
            if j == 0:
                outside = jnp.logical_or(outside, at_west)
            if j == 9:
                outside = jnp.logical_or(outside, at_east)
            image = jnp.where(outside, zero8, image)
            o = j * OROWS + 8 * tile
            image_ref[o : o + 8, :] = image
            change_ref[o : o + 8, :] = jnp.where(first_segment, image, zero8) - image

    left_out = jnp.logical_and(at_left, jnp.logical_and(rows_of(8) < 4, lo8))
    right_out = jnp.logical_and(at_right, jnp.logical_and(rows_of(8) >= 4, jnp.logical_not(lo8)))
    buffers = (a_ref, b_ref)
    for step in range(SUB):
        source = buffers[step % 2]
        target = buffers[(step + 1) % 2]
        last = step == SUB - 1
        begin = step + 1
        stop = 40 - begin
        if not last:
            for tile in range(9):

                def row_step(i, tile=tile, source=source, target=target):
                    r = i * FROWS + 8 + 8 * tile
                    value = advanced(
                        source[pl.ds(r, 8), :],
                        source[pl.ds(r + FROWS, 8), :],
                        source[pl.ds(r - FROWS, 8), :],
                        source[pl.ds(r + 1, 8), :],
                        source[pl.ds(r - 1, 8), :],
                        spread,
                    )
                    if tile == 0:
                        value = jnp.where(left_out, zero8, value)
                    if tile == 8:
                        value = jnp.where(right_out, zero8, value)
                    return r, value

                for i in range(begin, stop):
                    r, value = row_step(i)
                    if i < 4:
                        value = jnp.where(at_west, zero8, value)
                    if i >= 36:
                        value = jnp.where(at_east, zero8, value)
                    target[pl.ds(r, 8), :] = value
        else:
            for tile in range(8):
                for i in range(begin, stop):
                    r = i * FROWS + 12 + 8 * tile
                    value = advanced(
                        source[r : r + 8, :],
                        source[r + FROWS : r + FROWS + 8, :],
                        source[r - FROWS : r - FROWS + 8, :],
                        source[r + 1 : r + 9, :],
                        source[r - 1 : r + 7, :],
                        spread,
                    )
                    o = (i - 4) * HALF + 8 * tile
                    end_ref[o : o + 8, :] = value

    for j in range(CX):
        lower = change_ref[j * OROWS : (j + 1) * OROWS, :]
        middle = change_ref[(j + 1) * OROWS : (j + 2) * OROWS, :]
        upper = change_ref[(j + 2) * OROWS : (j + 3) * OROWS, :]
        blend_ref[...] = BLEND[0] * lower + BLEND[1] * middle + BLEND[2] * upper
        blended = (
            BLEND[0] * blend_ref[0:CY, :] + BLEND[1] * blend_ref[1 : CY + 1, :] + BLEND[2] * blend_ref[2 : CY + 2, :]
        )
        base = 4 * j * HALF
        sum_ref[0:HALF, :] = (end_ref[base : base + HALF, :] + end_ref[base + HALF : base + 2 * HALF, :]) + (
            end_ref[base + 2 * HALF : base + 3 * HALF, :] + end_ref[base + 3 * HALF : base + 4 * HALF, :]
        )
        part_ref[j * CY : (j + 1) * CY, :] = coarse_rows(sum_ref, 0, CY) + blended
    turned = part_ref[...].T
    for g in range(4):
        for h in range(2):
            send_ref[pl.ds(2 * g + h, LEVELS, stride=8), :] = turned[h * LEVELS : (h + 1) * LEVELS]


def chain_kernel(place_ref, diffuse_ref, wind_ref, part_ref, send_ref, pad_ref):
    level = place_ref[0] * 8 + place_ref[1]
    gy = place_ref[2]
    spread = (0.25 * STEP) * diffuse_ref[level]
    along_x = (0.5 * STEP) * wind_ref[0, level]
    along_y = (0.5 * STEP) * wind_ref[1, level]

    lane = lanes(64)
    row = rows_of(64)
    block = row % 8
    column = lane % 16
    zero = jnp.zeros((64, W), F32)

    def shifted(value):
        turned = pltpu.roll(value, W - 16, 1)
        following = jnp.where(row < 56, pltpu.roll(turned, 56, 0), zero)
        east = jnp.where(lane < W - 16, turned, following)
        turned = pltpu.roll(value, 16, 1)
        previous = jnp.where(row >= 8, pltpu.roll(turned, 8, 0), zero)
        west = jnp.where(lane >= 16, turned, previous)
        return east, west

    def shifted_y(value):
        following = jnp.where(block < 7, pltpu.roll(value, 63, 0), zero)
        north = jnp.where(column < 15, pltpu.roll(value, W - 1, 1), pltpu.roll(following, 15, 1))
        previous = jnp.where(block > 0, pltpu.roll(value, 1, 0), zero)
        south = jnp.where(column > 0, pltpu.roll(value, 1, 1), pltpu.roll(previous, W - 15, 1))
        return north, south

    pad_ref[...] = jnp.zeros_like(pad_ref)
    for r in range(3):
        send_ref[pl.ds(r, 8, stride=3), :] = jnp.zeros((8, W), F32)

    lane8 = lanes(8)
    item = lane8 % 64
    west_east = jnp.where(item < 16, item + 112, item - 16)
    west_east = jnp.where(item < 32, west_east, 0)
    left_column = item - 33
    right_column = item - 49
    side = jnp.where(item < 48, left_column * 16 + 15, right_column * 16)
    side = jnp.clip(side, 0, W - 1)

    coarse = part_ref[0:64, :]
    for n in range(1, 8):
        east, west = shifted(coarse)
        north, south = shifted_y(coarse)
        slope = along_x * (east - west) + along_y * (north - south)
        image = coarse + (spread * ((east + west) + (north + south) - 4.0 * coarse) - coarse * slope)
        for g in range(8):
            start = (g + 1) * 24 + 8
            pad_ref[start : start + 8, :] = image[8 * g : 8 * g + 8]

        def tiles(dx, b):
            return pad_ref[pl.ds((1 + dx) * 24 + 8 + b, 8, stride=24), :]

        b = 2 * gy
        rows = []
        for h in range(2):
            ends = jnp.where(lane8 >= 64, tiles(-1, b + h), tiles(1, b + h))
            ends = jnp.take_along_axis(ends, west_east, axis=1)
            sides = []
            for away in (-1, 1):
                own = jnp.take_along_axis(tiles(0, b + h + away), side, axis=1)
                at = 15 if away < 0 else 0
                lower = jnp.take_along_axis(tiles(-1, b + h + away), jnp.full((8, W), 112 + at, jnp.int32), axis=1)
                upper = jnp.take_along_axis(tiles(1, b + h + away), jnp.full((8, W), at, jnp.int32), axis=1)
                first = 32 if away < 0 else 48
                value = jnp.where(item == first, lower, jnp.where(item == first + 9, upper, own))
                sides.append(value)
            rows.append(jnp.where(item < 32, ends, jnp.where(item < 48, sides[0], sides[1])))
        base = n * 24
        send_ref[pl.ds(base, 8, stride=3), :] = tiles(0, b)
        send_ref[pl.ds(base + 1, 8, stride=3), :] = tiles(0, b + 1)
        send_ref[pl.ds(base + 2, 8, stride=3), :] = jnp.where(lane8 < 64, rows[0], rows[1])

        if n < 7:
            east, west = shifted(image)
            blended = BLEND[0] * west + BLEND[1] * image + BLEND[2] * east
            north, south = shifted_y(blended)
            blended = BLEND[0] * south + BLEND[1] * blended + BLEND[2] * north
            coarse = part_ref[n * 64 : (n + 1) * 64, :] + blended


def end_kernel(place_ref, end_ref, image_ref, back_ref, out_ref, change_ref, along_ref, fine_ref, turn_ref):
    first_segment = place_ref[0] == 0
    lo8 = low(8)
    main = jnp.concatenate(
        [back_ref[pl.ds(0, LEVELS, stride=3), :], back_ref[pl.ds(1, LEVELS, stride=3), :]], axis=0
    ).T
    ring = back_ref[pl.ds(2, LEVELS, stride=3), :]
    ring = jnp.concatenate([ring, ring], axis=0).T
    ring = jnp.where(low(64), ring[:64], ring[64:])

    change_ref[...] = jnp.zeros_like(change_ref)
    for j in range(10):
        start = j * OROWS
        if j == 0:
            rows = ring[0:16]
        elif j == 9:
            rows = ring[16:32]
        else:
            rows = main[(j - 1) * CY : j * CY]
        change_ref[start + 1 : start + 17, :] = rows
        change_ref[start : start + 1, :] = ring[32 + j : 33 + j]
        change_ref[start + 17 : start + 18, :] = ring[48 + j : 49 + j]
    for tile in range(10 * OROWS // 8):
        part = slice(8 * tile, 8 * tile + 8)
        image = image_ref[part, :]
        change_ref[part, :] = jnp.where(first_segment, image, change_ref[part, :]) - image

    lo = low(HALF)
    for j in range(CX):
        lower = change_ref[j * OROWS : (j + 1) * OROWS, :]
        middle = change_ref[(j + 1) * OROWS : (j + 2) * OROWS, :]
        upper = change_ref[(j + 2) * OROWS : (j + 3) * OROWS, :]
        for offset in range(4):
            along = WEIGHTS_MID[offset] * middle
            if offset < 2:
                along = along + WEIGHTS_LOW[offset] * lower
            else:
                along = along + WEIGHTS_HIGH[offset] * upper
            slot = offset * OROWS
            along_ref[slot : slot + OROWS, :] = along
            before = along_ref[slot : slot + CY, :]
            centre = along_ref[slot + 1 : slot + CY + 1, :]
            after = along_ref[slot + 2 : slot + CY + 2, :]
            for k in range(4):
                value = WEIGHTS_MID[k] * centre
                if k < 2:
                    value = value + WEIGHTS_LOW[k] * before
                else:
                    value = value + WEIGHTS_HIGH[k] * after
                fine_ref[pl.ds(offset * HALF + k, CY, stride=4), :] = value
        for pair in range(2):
            x = 4 * j + 2 * pair
            one = end_ref[x * HALF : (x + 1) * HALF, :] + fine_ref[2 * pair * HALF : (2 * pair + 1) * HALF, :]
            two = (
                end_ref[(x + 1) * HALF : (x + 2) * HALF, :]
                + fine_ref[(2 * pair + 1) * HALF : (2 * pair + 2) * HALF, :]
            )
            both = jnp.concatenate([jnp.where(lo, one, swap(two)), jnp.where(lo, swap(one), two)], axis=0).T
            out_ref[pl.ds(x, LEVELS, stride=NX), :] = both[:LEVELS]
            out_ref[pl.ds(x + 1, LEVELS, stride=NX), :] = both[LEVELS:]


def shape(rows):
    return jax.ShapeDtypeStruct((rows, W), F32)


VMEM = pl.BlockSpec(memory_space=pltpu.VMEM)
SMEM = pl.BlockSpec(memory_space=pltpu.SMEM)


def scratch(rows):
    return pltpu.VMEM((rows, W), F32)


def call(kernel, out_shape, in_specs, scratch_shapes, name):
    many = isinstance(out_shape, tuple)
    return pl.pallas_call(
        kernel,
        out_shape=out_shape,
        in_specs=in_specs,
        out_specs=(VMEM,) * len(out_shape) if many else VMEM,
        scratch_shapes=scratch_shapes,
        compiler_params=pltpu.CompilerParams(vmem_limit_bytes=24 * 1024 * 1024),
        name=name,
    )


def ring(array, axis, distance):
    devices = lax.axis_size(axis)
    return lax.ppermute(array, axis, [(i, (i + distance) % devices) for i in range(devices)])


def shards(state_starts, diffusivity, wind):
    place = jnp.stack([lax.axis_index(axis) for axis in ("tm", "gx", "gy")]).astype(jnp.int32)
    field = state_starts.reshape(LEVELS * NX, W)
    turned, first_rows, last_rows = call(
        pack_kernel, (shape(NX * HALF), shape(STRIP), shape(STRIP)), [VMEM], [scratch(HALF)], "pack"
    )(field)
    west = ring(last_rows, "gx", 1)
    east = ring(first_rows, "gx", -1)
    first_columns, last_columns = call(side_kernel, (shape(SIDE), shape(SIDE)), [VMEM] * 3, [], "sides")(
        turned, west, east
    )
    left = ring(last_columns, "gy", 1)
    right = ring(first_columns, "gy", -1)
    fine_end, image, parts = call(
        fine_kernel,
        (shape(NX * HALF), shape(10 * OROWS), shape(8 * LEVELS)),
        [SMEM] + [VMEM] * 7,
        [
            scratch(40 * FROWS), scratch(40 * FROWS), scratch(FROWS), scratch(12 * CROWS),
            scratch(10 * OROWS), scratch(OROWS), scratch(W),
        ],
        "fine",
    )(place, turned, west, east, left, right, diffusivity.reshape(1, LEVELS), wind)
    parts = lax.all_to_all(parts.reshape(256, 2, W), ("tm", "gx", "gy"), 0, 0, tiled=True)
    images = call(chain_kernel, shape(3 * 64), [SMEM, SMEM, SMEM, VMEM], [scratch(10 * 24)], "chain")(
        place, diffusivity, wind, parts.reshape(512, W)
    )
    images = lax.all_to_all(images.reshape(64, 3, W), ("tm", "gx"), 0, 0, tiled=True)
    ending = call(
        end_kernel,
        shape(LEVELS * NX),
        [SMEM] + [VMEM] * 3,
        [scratch(10 * OROWS), scratch(4 * OROWS), scratch(4 * HALF), scratch(HALF)],
        "ending",
    )(place, fine_end, image, images.reshape(192, W))
    return ending.reshape(1, LEVELS, NX, W)


def solution(mesh):
    placed = (P("tm", None, "gx", "gy"), P(), P())
    return jax.shard_map(
        shards, mesh=mesh, in_specs=placed, out_specs=P("tm", None, "gx", "gy"), check_vma=False
    )
```

```python
import jax
import jax.numpy as jnp
from jax import lax
from jax.experimental import pallas as pl
from jax.experimental.pallas import tpu as pltpu
from jax.sharding import PartitionSpec as P

SUB = 4
STEP = 0.2
LEVELS = 64
NX = 32
HALF = 64
CX = NX // 4
CY = HALF // 4
W = 128
WEIGHTS_LOW = (0.375, 0.125, 0.0, 0.0)
WEIGHTS_MID = (0.625, 0.875, 0.875, 0.625)
WEIGHTS_HIGH = (0.0, 0.0, 0.125, 0.375)
BLEND = (0.125, 0.75, 0.125)
F32 = jnp.float32

STRIP = 4 * HALF + CY
SIDE = 20 * 8 + 8
FROWS = 88
CROWS = 40
OROWS = 24


def lanes(rows):
    return lax.broadcasted_iota(jnp.int32, (rows, W), 1)


def rows_of(rows):
    return lax.broadcasted_iota(jnp.int32, (rows, W), 0)


def low(rows):
    return lanes(rows) < LEVELS


def swap(value):
    return pltpu.roll(value, LEVELS, 1)


def coarse_rows(ref, start, count):
    total = ref[pl.ds(start, count, stride=4), :]
    for offset in range(1, 4):
        total = total + ref[pl.ds(start + offset, count, stride=4), :]
    return total * (1.0 / 16.0)


def pack_kernel(u_ref, t_ref, first_ref, last_ref, sum_ref):
    lo = low(HALF)
    for x in range(0, NX, 2):
        both = jnp.concatenate(
            [u_ref[pl.ds(x, LEVELS, stride=NX), :], u_ref[pl.ds(x + 1, LEVELS, stride=NX), :]], axis=0
        ).T
        top = both[:HALF]
        bottom = both[HALF:]
        t_ref[x * HALF : (x + 1) * HALF, :] = jnp.where(lo, top, swap(bottom))
        t_ref[(x + 1) * HALF : (x + 2) * HALF, :] = jnp.where(lo, swap(top), bottom)

    def row(x):
        return t_ref[x * HALF : (x + 1) * HALF, :]

    first_ref[: 4 * HALF, :] = t_ref[: 4 * HALF, :]
    sum_ref[...] = (row(4) + row(5)) + (row(6) + row(7))
    first_ref[4 * HALF :, :] = coarse_rows(sum_ref, 0, CY)
    last_ref[: 4 * HALF, :] = t_ref[(NX - 4) * HALF :, :]
    sum_ref[...] = (row(NX - 8) + row(NX - 7)) + (row(NX - 6) + row(NX - 5))
    last_ref[4 * HALF :, :] = coarse_rows(sum_ref, 0, CY)


def side_kernel(t_ref, west_ref, east_ref, left_ref, right_ref):
    lo = low(8)

    def edge(x, start):
        if x < 0:
            base = (x + 4) * HALF
            return west_ref[base + start : base + start + 8, :]
        if x >= NX:
            base = (x - NX) * HALF
            return east_ref[base + start : base + start + 8, :]
        return t_ref[x * HALF + start : x * HALF + start + 8, :]

    for i in range(20):
        left_ref[8 * i : 8 * i + 8, :] = jnp.where(lo, edge(i - 4, 0), swap(edge(i + 16, 0)))
        right_ref[8 * i : 8 * i + 8, :] = jnp.where(
            lo, swap(edge(i - 4, HALF - 8)), edge(i + 16, HALF - 8)
        )
    base = 4 * HALF
    left_ref[160:168, :] = jnp.where(lo, west_ref[base : base + 8, :], swap(east_ref[base : base + 8, :]))
    right_ref[160:168, :] = jnp.where(
        lo, swap(west_ref[base + 8 : base + 16, :]), east_ref[base + 8 : base + 16, :]
    )


def both_halves(values):
    return jnp.concatenate([values, values], axis=1)


def fine_kernel(
    place_ref, t_ref, west_ref, east_ref, left_ref, right_ref, diffuse_ref, wind_ref,
    end_ref, image_ref, send_ref,
    a_ref, b_ref, sum_ref, coarse_ref, change_ref, blend_ref, part_ref,
):
    first_segment = place_ref[0] == 0
    at_west = place_ref[1] == 0
    at_east = place_ref[1] == 7
    at_left = place_ref[2] == 0
    at_right = place_ref[2] == 3
    lo8 = low(8)
    zero8 = jnp.zeros((8, W), F32)

    for i in range(40):
        x = i - 4
        if x < 0:
            source, base, outside = west_ref, (x + 4) * HALF, at_west
        elif x >= NX:
            source, base, outside = east_ref, (x - NX) * HALF, at_east
        else:
            source, base, outside = t_ref, x * HALF, None
        rows = source[base : base + HALF, :]
        j = i % 20
        from_left = left_ref[8 * j : 8 * j + 8, :]
        from_right = right_ref[8 * j : 8 * j + 8, :]
        if i >= 20:
            from_left = swap(from_left)
        else:
            from_right = swap(from_right)
        from_left = jnp.where(at_left, zero8, from_left)
        from_right = jnp.where(at_right, zero8, from_right)
        before = jnp.where(lo8, from_left, swap(rows[HALF - 8 :]))
        after = jnp.where(lo8, swap(rows[:8]), from_right)
        if outside is not None:
            rows = jnp.where(outside, jnp.zeros_like(rows), rows)
            before = jnp.where(outside, zero8, before)
            after = jnp.where(outside, zero8, after)
        start = i * FROWS
        a_ref[start : start + 4, :] = zero8[:4]
        a_ref[start + 4 : start + 12, :] = before
        a_ref[start + 12 : start + 76, :] = rows
        a_ref[start + 76 : start + 84, :] = after
        a_ref[start + 84 : start + 88, :] = zero8[:4]

    diffuse = both_halves(diffuse_ref[...])
    wind = both_halves(wind_ref[...])
    spread = jnp.broadcast_to(STEP * diffuse, (8, W))
    along_x = jnp.broadcast_to((0.5 * STEP) * wind[0:1], (8, W))
    along_y = jnp.broadcast_to((0.5 * STEP) * wind[1:2], (8, W))

    def advanced(centre, east, west, north, south, kd):
        slope = along_x * (east - west) + along_y * (north - south)
        return centre + (kd * ((east + west) + (north + south) - 4.0 * centre) - centre * slope)

    coarse_ref[...] = jnp.zeros_like(coarse_ref)
    for j in range(10):
        base = 4 * j * FROWS
        sum_ref[...] = (a_ref[base : base + FROWS, :] + a_ref[base + FROWS : base + 2 * FROWS, :]) + (
            a_ref[base + 2 * FROWS : base + 3 * FROWS, :] + a_ref[base + 3 * FROWS : base + 4 * FROWS, :]
        )
        start = (j + 1) * CROWS
        coarse_ref[start + 7 : start + 27, :] = coarse_rows(sum_ref, 4, 20)
    left_corner = left_ref[160:168, :]
    right_corner = right_ref[160:168, :]
    for source, start, outside, is_west in (
        (west_ref, 0, at_west, True),
        (east_ref, 11 * CROWS, at_east, False),
    ):
        rows = source[4 * HALF :, :]
        from_left = left_corner if is_west else swap(left_corner)
        from_right = swap(right_corner) if is_west else right_corner
        from_left = jnp.where(at_left, zero8, from_left)
        from_right = jnp.where(at_right, zero8, from_right)
        before = jnp.where(lo8, from_left, swap(rows[8:]))
        after = jnp.where(lo8, swap(rows[:8]), from_right)
        coarse_ref[start + 1 : start + 9, :] = jnp.where(outside, zero8, before)
        coarse_ref[start + 9 : start + 25, :] = jnp.where(outside, jnp.zeros_like(rows), rows)
        coarse_ref[start + 25 : start + 33, :] = jnp.where(outside, zero8, after)

    for j in range(10):
        for tile in range(3):
            r = (j + 1) * CROWS + 8 + 8 * tile
            image = advanced(
                coarse_ref[r : r + 8, :],
                coarse_ref[r + CROWS : r + CROWS + 8, :],
                coarse_ref[r - CROWS : r - CROWS + 8, :],
                coarse_ref[r + 1 : r + 9, :],
                coarse_ref[r - 1 : r + 7, :],
                0.25 * spread,
            )
            cy = rows_of(8) + (8 * tile - 1)
            outside = cy > CY
            if tile == 0:
                outside = jnp.logical_or(outside, jnp.logical_and(at_left, jnp.logical_and(cy < 0, lo8)))
            if tile == 2:
                outside = jnp.logical_or(
                    outside, jnp.logical_and(at_right, jnp.logical_and(cy >= CY, jnp.logical_not(lo8)))
                )
            if j == 0:
                outside = jnp.logical_or(outside, at_west)
            if j == 9:
                outside = jnp.logical_or(outside, at_east)
            image = jnp.where(outside, zero8, image)
            o = j * OROWS + 8 * tile
            image_ref[o : o + 8, :] = image
            change_ref[o : o + 8, :] = jnp.where(first_segment, image, zero8) - image

    left_out = jnp.logical_and(at_left, jnp.logical_and(rows_of(8) < 4, lo8))
    right_out = jnp.logical_and(at_right, jnp.logical_and(rows_of(8) >= 4, jnp.logical_not(lo8)))
    buffers = (a_ref, b_ref)
    for step in range(SUB):
        source = buffers[step % 2]
        target = buffers[(step + 1) % 2]
        last = step == SUB - 1
        begin = step + 1
        stop = 40 - begin
        if not last:
            for tile in range(9):

                def row_step(i, tile=tile, source=source, target=target):
                    r = i * FROWS + 8 + 8 * tile
                    value = advanced(
                        source[pl.ds(r, 8), :],
                        source[pl.ds(r + FROWS, 8), :],
                        source[pl.ds(r - FROWS, 8), :],
                        source[pl.ds(r + 1, 8), :],
                        source[pl.ds(r - 1, 8), :],
                        spread,
                    )
                    if tile == 0:
                        value = jnp.where(left_out, zero8, value)
                    if tile == 8:
                        value = jnp.where(right_out, zero8, value)
                    return r, value

                for i in range(begin, stop):
                    r, value = row_step(i)
                    if i < 4:
                        value = jnp.where(at_west, zero8, value)
                    if i >= 36:
                        value = jnp.where(at_east, zero8, value)
                    target[pl.ds(r, 8), :] = value
        else:
            for tile in range(8):
                for i in range(begin, stop):
                    r = i * FROWS + 12 + 8 * tile
                    value = advanced(
                        source[r : r + 8, :],
                        source[r + FROWS : r + FROWS + 8, :],
                        source[r - FROWS : r - FROWS + 8, :],
                        source[r + 1 : r + 9, :],
                        source[r - 1 : r + 7, :],
                        spread,
                    )
                    o = (i - 4) * HALF + 8 * tile
                    end_ref[o : o + 8, :] = value

    for j in range(CX):
        lower = change_ref[j * OROWS : (j + 1) * OROWS, :]
        middle = change_ref[(j + 1) * OROWS : (j + 2) * OROWS, :]
        upper = change_ref[(j + 2) * OROWS : (j + 3) * OROWS, :]
        blend_ref[...] = BLEND[0] * lower + BLEND[1] * middle + BLEND[2] * upper
        blended = (
            BLEND[0] * blend_ref[0:CY, :] + BLEND[1] * blend_ref[1 : CY + 1, :] + BLEND[2] * blend_ref[2 : CY + 2, :]
        )
        base = 4 * j * HALF
        sum_ref[0:HALF, :] = (end_ref[base : base + HALF, :] + end_ref[base + HALF : base + 2 * HALF, :]) + (
            end_ref[base + 2 * HALF : base + 3 * HALF, :] + end_ref[base + 3 * HALF : base + 4 * HALF, :]
        )
        part_ref[j * CY : (j + 1) * CY, :] = coarse_rows(sum_ref, 0, CY) + blended
    turned = part_ref[...].T
    for h in range(2):
        send_ref[pl.ds(h, LEVELS, stride=2), :] = turned[h * LEVELS : (h + 1) * LEVELS]


def split_kernel(part_ref, first_ref, second_ref):
    first_ref[...] = part_ref[pl.ds(0, LEVELS, stride=2), :]
    second_ref[...] = part_ref[pl.ds(1, LEVELS, stride=2), :]


def chain_kernel(place_ref, diffuse_ref, wind_ref, part_ref, left_ref, right_ref, send_ref):
    level = place_ref[0] * 8 + place_ref[1]
    at_left = place_ref[2] == 0
    at_right = place_ref[2] == 3
    spread = (0.25 * STEP) * diffuse_ref[level]
    along_x = (0.5 * STEP) * wind_ref[0, level]
    along_y = (0.5 * STEP) * wind_ref[1, level]

    lane = lanes(8)
    row = rows_of(8)
    column = lane % 16
    zero = jnp.zeros((8, W), F32)

    def neighbours(tile):
        up = jnp.where(row < 7, pltpu.roll(tile, 7, 0), zero)
        down = jnp.where(row > 0, pltpu.roll(tile, 1, 0), zero)
        return up, down

    def along_rows(tile, up, down):
        east = pltpu.roll(jnp.where(lane < 16, up, tile), W - 16, 1)
        west = pltpu.roll(jnp.where(lane >= W - 16, down, tile), 16, 1)
        return east, west

    def along_columns(tiles):
        after = [pltpu.roll(tile, W - 1, 1) for tile in tiles]
        before = [pltpu.roll(tile, 1, 1) for tile in tiles]
        after_far = [pltpu.roll(tile, 15, 1) for tile in tiles[1:]] + [zero]
        before_far = [zero] + [pltpu.roll(tile, W - 15, 1) for tile in tiles[:-1]]
        north = [jnp.where(column < 15, near, far) for near, far in zip(after, after_far)]
        south = [jnp.where(column > 0, near, far) for near, far in zip(before, before_far)]
        return north, south

    def cleared(tiles):
        return [jnp.where(at_left, zero, tiles[0]), tiles[1], tiles[2], jnp.where(at_right, zero, tiles[3])]

    def part(n):
        return cleared(
            [
                left_ref[8 * n : 8 * n + 8, :],
                part_ref[pl.ds(16 * n, 8, stride=2), :],
                part_ref[pl.ds(16 * n + 1, 8, stride=2), :],
                right_ref[8 * n : 8 * n + 8, :],
            ]
        )

    item = lane % 64
    end_lane = jnp.where(item < 16, item + (W - 16), jnp.where(item < 32, item - 16, 0))
    side_lane = jnp.clip(jnp.where(item < 48, (item - 33) * 16 + 15, (item - 49) * 16), 0, W - 1)
    corner_lane = jnp.where(item < 40, W - 1, jnp.where(item < 45, 15, jnp.where(item < 52, W - 16, 0)))
    is_corner = (item == 32) | (item == 41) | (item == 48) | (item == 57)

    def picked(values, index):
        return jnp.take_along_axis(values, index, axis=1)

    for r in range(3):
        send_ref[pl.ds(r, 8, stride=3), :] = zero
    coarse = part(0)
    for n in range(1, 8):
        north, south = along_columns(coarse)
        image = []
        for b in range(4):
            east, west = along_rows(coarse[b], *neighbours(coarse[b]))
            slope = along_x * (east - west) + along_y * (north[b] - south[b])
            total = (east + west) + (north[b] + south[b])
            image.append(coarse[b] + (spread * (total - 4.0 * coarse[b]) - coarse[b] * slope))
        image = cleared(image)
        beside = [neighbours(tile) for tile in image]

        rows = []
        for b in (1, 2):
            ends = picked(jnp.where(lane >= 64, beside[b][1], beside[b][0]), end_lane)
            sides = picked(jnp.where(column == 15, image[b - 1], image[b + 1]), side_lane)
            corners = jnp.where(
                lane >= 64,
                jnp.where(column == 15, beside[b - 1][1], beside[b + 1][1]),
                jnp.where(column == 15, beside[b - 1][0], beside[b + 1][0]),
            )
            corners = picked(corners, corner_lane)
            rows.append(jnp.where(item < 32, ends, jnp.where(is_corner, corners, sides)))
        base = n * 24
        send_ref[pl.ds(base, 8, stride=3), :] = image[1]
        send_ref[pl.ds(base + 1, 8, stride=3), :] = image[2]
        send_ref[pl.ds(base + 2, 8, stride=3), :] = jnp.where(lane < 64, rows[0], rows[1])

        if n < 7:
            blended = []
            for tile, pair in zip(image, beside):
                east, west = along_rows(tile, *pair)
                blended.append(BLEND[0] * west + BLEND[1] * tile + BLEND[2] * east)
            north, south = along_columns(blended)
            coarse = cleared(
                [
                    value + (BLEND[0] * s + BLEND[1] * tile + BLEND[2] * n_)
                    for value, s, tile, n_ in zip(part(n), south, blended, north)
                ]
            )


def end_kernel(place_ref, end_ref, image_ref, back_ref, out_ref, change_ref, along_ref, fine_ref, turn_ref):
    first_segment = place_ref[0] == 0
    lo8 = low(8)
    main = jnp.concatenate(
        [back_ref[pl.ds(0, LEVELS, stride=3), :], back_ref[pl.ds(1, LEVELS, stride=3), :]], axis=0
    ).T
    ring = back_ref[pl.ds(2, LEVELS, stride=3), :]
    ring = jnp.concatenate([ring, ring], axis=0).T
    ring = jnp.where(low(64), ring[:64], ring[64:])

    change_ref[...] = jnp.zeros_like(change_ref)
    for j in range(10):
        start = j * OROWS
        if j == 0:
            rows = ring[0:16]
        elif j == 9:
            rows = ring[16:32]
        else:
            rows = main[(j - 1) * CY : j * CY]
        change_ref[start + 1 : start + 17, :] = rows
        change_ref[start : start + 1, :] = ring[32 + j : 33 + j]
        change_ref[start + 17 : start + 18, :] = ring[48 + j : 49 + j]
    for tile in range(10 * OROWS // 8):
        part = slice(8 * tile, 8 * tile + 8)
        image = image_ref[part, :]
        change_ref[part, :] = jnp.where(first_segment, image, change_ref[part, :]) - image

    lo = low(HALF)
    for j in range(CX):
        lower = change_ref[j * OROWS : (j + 1) * OROWS, :]
        middle = change_ref[(j + 1) * OROWS : (j + 2) * OROWS, :]
        upper = change_ref[(j + 2) * OROWS : (j + 3) * OROWS, :]
        for offset in range(4):
            along = WEIGHTS_MID[offset] * middle
            if offset < 2:
                along = along + WEIGHTS_LOW[offset] * lower
            else:
                along = along + WEIGHTS_HIGH[offset] * upper
            slot = offset * OROWS
            along_ref[slot : slot + OROWS, :] = along
            before = along_ref[slot : slot + CY, :]
            centre = along_ref[slot + 1 : slot + CY + 1, :]
            after = along_ref[slot + 2 : slot + CY + 2, :]
            for k in range(4):
                value = WEIGHTS_MID[k] * centre
                if k < 2:
                    value = value + WEIGHTS_LOW[k] * before
                else:
                    value = value + WEIGHTS_HIGH[k] * after
                fine_ref[pl.ds(offset * HALF + k, CY, stride=4), :] = value
        for pair in range(2):
            x = 4 * j + 2 * pair
            one = end_ref[x * HALF : (x + 1) * HALF, :] + fine_ref[2 * pair * HALF : (2 * pair + 1) * HALF, :]
            two = (
                end_ref[(x + 1) * HALF : (x + 2) * HALF, :]
                + fine_ref[(2 * pair + 1) * HALF : (2 * pair + 2) * HALF, :]
            )
            both = jnp.concatenate([jnp.where(lo, one, swap(two)), jnp.where(lo, swap(one), two)], axis=0).T
            out_ref[pl.ds(x, LEVELS, stride=NX), :] = both[:LEVELS]
            out_ref[pl.ds(x + 1, LEVELS, stride=NX), :] = both[LEVELS:]


def shape(rows):
    return jax.ShapeDtypeStruct((rows, W), F32)


VMEM = pl.BlockSpec(memory_space=pltpu.VMEM)
SMEM = pl.BlockSpec(memory_space=pltpu.SMEM)


def scratch(rows):
    return pltpu.VMEM((rows, W), F32)


def call(kernel, out_shape, in_specs, scratch_shapes, name):
    many = isinstance(out_shape, tuple)
    return pl.pallas_call(
        kernel,
        out_shape=out_shape,
        in_specs=in_specs,
        out_specs=(VMEM,) * len(out_shape) if many else VMEM,
        scratch_shapes=scratch_shapes,
        compiler_params=pltpu.CompilerParams(vmem_limit_bytes=24 * 1024 * 1024),
        name=name,
    )


def ring(array, axis, distance):
    devices = lax.axis_size(axis)
    return lax.ppermute(array, axis, [(i, (i + distance) % devices) for i in range(devices)])


def shards(state_starts, diffusivity, wind):
    place = jnp.stack([lax.axis_index(axis) for axis in ("tm", "gx", "gy")]).astype(jnp.int32)
    field = state_starts.reshape(LEVELS * NX, W)
    turned, first_rows, last_rows = call(
        pack_kernel, (shape(NX * HALF), shape(STRIP), shape(STRIP)), [VMEM], [scratch(HALF)], "pack"
    )(field)
    west = ring(last_rows, "gx", 1)
    east = ring(first_rows, "gx", -1)
    first_columns, last_columns = call(side_kernel, (shape(SIDE), shape(SIDE)), [VMEM] * 3, [], "sides")(
        turned, west, east
    )
    left = ring(last_columns, "gy", 1)
    right = ring(first_columns, "gy", -1)
    fine_end, image, parts = call(
        fine_kernel,
        (shape(NX * HALF), shape(10 * OROWS), shape(2 * LEVELS)),
        [SMEM] + [VMEM] * 7,
        [
            scratch(40 * FROWS), scratch(40 * FROWS), scratch(FROWS), scratch(12 * CROWS),
            scratch(10 * OROWS), scratch(OROWS), scratch(W),
        ],
        "fine",
    )(place, turned, west, east, left, right, diffusivity.reshape(1, LEVELS), wind)
    parts = lax.all_to_all(parts.reshape(LEVELS, 2, W), ("tm", "gx"), 0, 0, tiled=True).reshape(2 * LEVELS, W)
    first_half, second_half = call(split_kernel, (shape(LEVELS), shape(LEVELS)), [VMEM], [], "split")(parts)
    left = ring(second_half, "gy", 1)
    right = ring(first_half, "gy", -1)
    images = call(chain_kernel, shape(3 * LEVELS), [SMEM] * 3 + [VMEM] * 3, [], "chain")(
        place, diffusivity, wind, parts, left, right
    )
    images = lax.all_to_all(images.reshape(LEVELS, 3, W), ("tm", "gx"), 0, 0, tiled=True)
    ending = call(
        end_kernel,
        shape(LEVELS * NX),
        [SMEM] + [VMEM] * 3,
        [scratch(10 * OROWS), scratch(4 * OROWS), scratch(4 * HALF), scratch(HALF)],
        "ending",
    )(place, fine_end, image, images.reshape(192, W))
    return ending.reshape(1, LEVELS, NX, W)


def solution(mesh):
    placed = (P("tm", None, "gx", "gy"), P(), P())
    return jax.shard_map(
        shards, mesh=mesh, in_specs=placed, out_specs=P("tm", None, "gx", "gy"), check_vma=False
    )
```

```python
import jax
import jax.numpy as jnp
import ml_dtypes
import numpy as np
from jax import lax
from jax.experimental import pallas as pl
from jax.experimental.pallas import tpu as pltpu
from jax.sharding import PartitionSpec as P

SUB = 4
STEP = 0.2
LEVELS = 64
NX = 32
HALF = 64
CX = NX // 4
CY = HALF // 4
W = 128
WEIGHTS_LOW = (0.375, 0.125, 0.0, 0.0)
WEIGHTS_MID = (0.625, 0.875, 0.875, 0.625)
WEIGHTS_HIGH = (0.0, 0.0, 0.125, 0.375)
BLEND = (0.125, 0.75, 0.125)
F32 = jnp.float32

STRIP = 4 * HALF + CY
SIDE = 20 * 8 + 8
FROWS = 88
CROWS = 40
OROWS = 24


def lanes(rows):
    return lax.broadcasted_iota(jnp.int32, (rows, W), 1)


def rows_of(rows):
    return lax.broadcasted_iota(jnp.int32, (rows, W), 0)


def low(rows):
    return lanes(rows) < LEVELS


def swap(value):
    return pltpu.roll(value, LEVELS, 1)


def coarse_rows(ref, start, count):
    total = ref[pl.ds(start, count, stride=4), :]
    for offset in range(1, 4):
        total = total + ref[pl.ds(start + offset, count, stride=4), :]
    return total * (1.0 / 16.0)


def turned_pair(rows_ref, x, stride):
    lo = low(HALF)
    both = jnp.concatenate(
        [rows_ref[pl.ds(x, LEVELS, stride=stride), :], rows_ref[pl.ds(x + 1, LEVELS, stride=stride), :]], axis=0
    ).T
    top = both[:HALF]
    bottom = both[HALF:]
    return jnp.where(lo, top, swap(bottom)), jnp.where(lo, swap(top), bottom)


def edge_kernel(low_ref, high_ref, edge_ref, first_ref, last_ref, sum_ref):
    for side, (rows_ref, strip_ref) in enumerate(((low_ref, first_ref), (high_ref, last_ref))):
        rows = []
        for x in range(0, 8, 2):
            rows += turned_pair(rows_ref, x, 8)
        for x in range(8):
            base = (8 * side + x) * HALF
            edge_ref[base : base + HALF, :] = rows[x]
        near = rows[:4] if side == 0 else rows[4:]
        far = rows[4:] if side == 0 else rows[:4]
        for x in range(4):
            strip_ref[x * HALF : (x + 1) * HALF, :] = near[x]
        sum_ref[...] = (far[0] + far[1]) + (far[2] + far[3])
        strip_ref[4 * HALF :, :] = coarse_rows(sum_ref, 0, CY)


def middle_kernel(rows_ref, middle_ref):
    for x in range(0, 16, 2):
        one, two = turned_pair(rows_ref, x, 16)
        middle_ref[x * HALF : (x + 1) * HALF, :] = one
        middle_ref[(x + 1) * HALF : (x + 2) * HALF, :] = two


def block_row(x, edge_ref, middle_ref, west_ref, east_ref):
    if x < 0:
        return west_ref, (x + 4) * HALF
    if x >= NX:
        return east_ref, (x - NX) * HALF
    if x < 8:
        return edge_ref, x * HALF
    if x >= NX - 8:
        return edge_ref, (x - NX + 16) * HALF
    return middle_ref, (x - 8) * HALF


def side_kernel(edge_ref, middle_ref, west_ref, east_ref, left_ref, right_ref):
    lo = low(8)

    def edge(x, start):
        source, base = block_row(x, edge_ref, middle_ref, west_ref, east_ref)
        return source[base + start : base + start + 8, :]

    for i in range(20):
        left_ref[8 * i : 8 * i + 8, :] = jnp.where(lo, edge(i - 4, 0), swap(edge(i + 16, 0)))
        right_ref[8 * i : 8 * i + 8, :] = jnp.where(
            lo, swap(edge(i - 4, HALF - 8)), edge(i + 16, HALF - 8)
        )
    base = 4 * HALF
    left_ref[160:168, :] = jnp.where(lo, west_ref[base : base + 8, :], swap(east_ref[base : base + 8, :]))
    right_ref[160:168, :] = jnp.where(
        lo, swap(west_ref[base + 8 : base + 16, :]), east_ref[base + 8 : base + 16, :]
    )


def both_halves(values):
    return jnp.concatenate([values, values], axis=1)


def coefficients(diffuse_ref, wind_ref):
    diffuse = both_halves(diffuse_ref[...])
    wind = both_halves(wind_ref[...])
    spread = jnp.broadcast_to(STEP * diffuse, (8, W))
    along_x = jnp.broadcast_to((0.5 * STEP) * wind[0:1], (8, W))
    along_y = jnp.broadcast_to((0.5 * STEP) * wind[1:2], (8, W))
    return spread, along_x, along_y


def advanced(ref, r, rows, coefs, factor):
    spread, along_x, along_y = coefs
    centre = ref[r : r + 8, :]
    east = ref[r + rows : r + rows + 8, :]
    west = ref[r - rows : r - rows + 8, :]
    north = ref[r + 1 : r + 9, :]
    south = ref[r - 1 : r + 7, :]
    slope = along_x * (east - west) + along_y * (north - south)
    return centre + ((factor * spread) * ((east + west) + (north + south) - 4.0 * centre) - centre * slope)


def substeps(place_ref, states, end_ref, coefs, tiles, end_tiles):
    at_west = place_ref[1] == 0
    at_east = place_ref[1] == 7
    lo = low(8)
    zero8 = jnp.zeros((8, W), F32)
    left_out = jnp.logical_and(place_ref[2] == 0, jnp.logical_and(rows_of(8) < 4, lo))
    right_out = jnp.logical_and(place_ref[2] == 3, jnp.logical_and(rows_of(8) >= 4, jnp.logical_not(lo)))
    for step in range(SUB - 1):
        for tile in tiles:
            for i in range(step + 1, 39 - step):
                r = i * FROWS + 8 + 8 * tile
                value = advanced(states[step], r, FROWS, coefs, 1.0)
                if tile == 0:
                    value = jnp.where(left_out, zero8, value)
                if tile == 8:
                    value = jnp.where(right_out, zero8, value)
                if i < 4:
                    value = jnp.where(at_west, zero8, value)
                if i >= 36:
                    value = jnp.where(at_east, zero8, value)
                states[step + 1][r : r + 8, :] = value
    for tile in end_tiles:
        for i in range(4, 36):
            o = (i - 4) * HALF + 8 * tile
            end_ref[o : o + 8, :] = advanced(states[SUB - 1], i * FROWS + 12 + 8 * tile, FROWS, coefs, 1.0)


def inner_kernel(
    place_ref, edge_ref, middle_ref, west_ref, east_ref, diffuse_ref, wind_ref,
    s0_ref, s1_ref, s2_ref, s3_ref, end_ref, coarse_ref, sum_ref,
):
    lo8 = low(8)
    zero8 = jnp.zeros((8, W), F32)
    for i in range(40):
        source, base = block_row(i - 4, edge_ref, middle_ref, west_ref, east_ref)
        rows = source[base : base + HALF, :]
        before = jnp.where(lo8, zero8, swap(rows[HALF - 8 :]))
        after = jnp.where(lo8, swap(rows[:8]), zero8)
        if i < 4 or i >= 36:
            outside = place_ref[1] == (0 if i < 4 else 7)
            rows = jnp.where(outside, jnp.zeros_like(rows), rows)
            before = jnp.where(outside, zero8, before)
            after = jnp.where(outside, zero8, after)
        start = i * FROWS
        s0_ref[start : start + 4, :] = zero8[:4]
        s0_ref[start + 4 : start + 12, :] = before
        s0_ref[start + 12 : start + 76, :] = rows
        s0_ref[start + 76 : start + 84, :] = after
        s0_ref[start + 84 : start + 88, :] = zero8[:4]

    coarse_ref[...] = jnp.zeros_like(coarse_ref)
    for j in range(10):
        base = 4 * j * FROWS
        sum_ref[...] = (s0_ref[base : base + FROWS, :] + s0_ref[base + FROWS : base + 2 * FROWS, :]) + (
            s0_ref[base + 2 * FROWS : base + 3 * FROWS, :] + s0_ref[base + 3 * FROWS : base + 4 * FROWS, :]
        )
        start = (j + 1) * CROWS
        coarse_ref[start + 7 : start + 27, :] = coarse_rows(sum_ref, 4, 20)

    states = (s0_ref, s1_ref, s2_ref, s3_ref)
    substeps(place_ref, states, end_ref, coefficients(diffuse_ref, wind_ref), range(9), range(8))


def outer_kernel(
    place_ref, west_ref, east_ref, left_ref, right_ref, diffuse_ref, wind_ref,
    s0_in, s1_in, s2_in, s3_in, end_in, coarse_in,
    s0_ref, s1_ref, s2_ref, s3_ref, end_ref, coarse_ref, change_ref, send_ref,
    sum_ref, blend_ref, part_ref,
):
    del s0_in, s1_in, s2_in, s3_in, end_in, coarse_in
    first_segment = place_ref[0] == 0
    at_west = place_ref[1] == 0
    at_east = place_ref[1] == 7
    at_left = place_ref[2] == 0
    at_right = place_ref[2] == 3
    lo8 = low(8)
    zero8 = jnp.zeros((8, W), F32)
    coefs = coefficients(diffuse_ref, wind_ref)

    for j in range(10):
        befores = []
        afters = []
        for i in range(4 * j, 4 * j + 4):
            k = i % 20
            from_left = left_ref[8 * k : 8 * k + 8, :]
            from_right = right_ref[8 * k : 8 * k + 8, :]
            if i >= 20:
                from_left = swap(from_left)
            else:
                from_right = swap(from_right)
            start = i * FROWS
            known = s0_ref[start + 4 : start + 12, :]
            before = jnp.where(lo8, jnp.where(at_left, zero8, from_left), known)
            known = s0_ref[start + 76 : start + 84, :]
            after = jnp.where(lo8, known, jnp.where(at_right, zero8, from_right))
            if i < 4 or i >= 36:
                outside = at_west if i < 4 else at_east
                before = jnp.where(outside, zero8, before)
                after = jnp.where(outside, zero8, after)
            s0_ref[start + 4 : start + 12, :] = before
            s0_ref[start + 76 : start + 84, :] = after
            befores.append(before)
            afters.append(after)
        base = 16 * j
        sum_ref[base : base + 8, :] = (befores[0] + befores[1]) + (befores[2] + befores[3])
        sum_ref[base + 8 : base + 16, :] = (afters[0] + afters[1]) + (afters[2] + afters[3])
        start = (j + 1) * CROWS
        coarse_ref[start + 7 : start + 9, :] = coarse_rows(sum_ref, base, 2)
        coarse_ref[start + 25 : start + 27, :] = coarse_rows(sum_ref, base + 8, 2)
    left_corner = left_ref[160:168, :]
    right_corner = right_ref[160:168, :]
    for source, start, outside, is_west in (
        (west_ref, 0, at_west, True),
        (east_ref, 11 * CROWS, at_east, False),
    ):
        rows = source[4 * HALF :, :]
        from_left = left_corner if is_west else swap(left_corner)
        from_right = swap(right_corner) if is_west else right_corner
        from_left = jnp.where(at_left, zero8, from_left)
        from_right = jnp.where(at_right, zero8, from_right)
        before = jnp.where(lo8, from_left, swap(rows[8:]))
        after = jnp.where(lo8, swap(rows[:8]), from_right)
        coarse_ref[start + 1 : start + 9, :] = jnp.where(outside, zero8, before)
        coarse_ref[start + 9 : start + 25, :] = jnp.where(outside, jnp.zeros_like(rows), rows)
        coarse_ref[start + 25 : start + 33, :] = jnp.where(outside, zero8, after)

    for j in range(10):
        for tile in range(3):
            image = advanced(coarse_ref, (j + 1) * CROWS + 8 + 8 * tile, CROWS, coefs, 0.25)
            cy = rows_of(8) + (8 * tile - 1)
            outside = cy > CY
            if tile == 0:
                outside = jnp.logical_or(outside, jnp.logical_and(at_left, jnp.logical_and(cy < 0, lo8)))
            if tile == 2:
                outside = jnp.logical_or(
                    outside, jnp.logical_and(at_right, jnp.logical_and(cy >= CY, jnp.logical_not(lo8)))
                )
            if j == 0:
                outside = jnp.logical_or(outside, at_west)
            if j == 9:
                outside = jnp.logical_or(outside, at_east)
            image = jnp.where(outside, zero8, image)
            o = j * OROWS + 8 * tile
            change_ref[o : o + 8, :] = jnp.where(first_segment, image, zero8) - image

    states = (s0_ref, s1_ref, s2_ref, s3_ref)
    substeps(place_ref, states, end_ref, coefs, (0, 8), (0, 7))

    for j in range(CX):
        lower = change_ref[j * OROWS : (j + 1) * OROWS, :]
        middle = change_ref[(j + 1) * OROWS : (j + 2) * OROWS, :]
        upper = change_ref[(j + 2) * OROWS : (j + 3) * OROWS, :]
        slot = j * OROWS
        blend_ref[slot : slot + OROWS, :] = BLEND[0] * lower + BLEND[1] * middle + BLEND[2] * upper
        blended = (
            BLEND[0] * blend_ref[slot : slot + CY, :]
            + BLEND[1] * blend_ref[slot + 1 : slot + CY + 1, :]
            + BLEND[2] * blend_ref[slot + 2 : slot + CY + 2, :]
        )
        base = 4 * j * HALF
        total = (end_ref[base : base + HALF, :] + end_ref[base + HALF : base + 2 * HALF, :]) + (
            end_ref[base + 2 * HALF : base + 3 * HALF, :] + end_ref[base + 3 * HALF : base + 4 * HALF, :]
        )
        spot = 160 + j * HALF
        sum_ref[spot : spot + HALF, :] = total
        part_ref[j * CY : (j + 1) * CY, :] = coarse_rows(sum_ref, spot, CY) + blended
    turned = part_ref[...].T
    for h in range(2):
        send_ref[pl.ds(h, LEVELS, stride=2), :] = turned[h * LEVELS : (h + 1) * LEVELS]


def split_kernel(part_ref, first_ref, second_ref):
    first_ref[...] = part_ref[pl.ds(0, LEVELS, stride=2), :]
    second_ref[...] = part_ref[pl.ds(1, LEVELS, stride=2), :]


def chain_kernel(place_ref, diffuse_ref, wind_ref, part_ref, left_ref, right_ref, send_ref):
    level = place_ref[0] * 8 + place_ref[1]
    at_left = place_ref[2] == 0
    at_right = place_ref[2] == 3
    spread = (0.25 * STEP) * diffuse_ref[level]
    along_x = (0.5 * STEP) * wind_ref[0, level]
    along_y = (0.5 * STEP) * wind_ref[1, level]

    lane = lanes(8)
    row = rows_of(8)
    column = lane % 16
    zero = jnp.zeros((8, W), F32)

    def neighbours(tile):
        up = jnp.where(row < 7, pltpu.roll(tile, 7, 0), zero)
        down = jnp.where(row > 0, pltpu.roll(tile, 1, 0), zero)
        return up, down

    def along_rows(tile, up, down):
        east = pltpu.roll(jnp.where(lane < 16, up, tile), W - 16, 1)
        west = pltpu.roll(jnp.where(lane >= W - 16, down, tile), 16, 1)
        return east, west

    def along_columns(tiles):
        after = [pltpu.roll(tile, W - 1, 1) for tile in tiles]
        before = [pltpu.roll(tile, 1, 1) for tile in tiles]
        after_far = [pltpu.roll(tile, 15, 1) for tile in tiles[1:]] + [zero]
        before_far = [zero] + [pltpu.roll(tile, W - 15, 1) for tile in tiles[:-1]]
        north = [jnp.where(column < 15, near, far) for near, far in zip(after, after_far)]
        south = [jnp.where(column > 0, near, far) for near, far in zip(before, before_far)]
        return north, south

    def cleared(tiles):
        return [jnp.where(at_left, zero, tiles[0]), tiles[1], tiles[2], jnp.where(at_right, zero, tiles[3])]

    def part(n):
        return cleared(
            [
                left_ref[8 * n : 8 * n + 8, :],
                part_ref[pl.ds(16 * n, 8, stride=2), :],
                part_ref[pl.ds(16 * n + 1, 8, stride=2), :],
                right_ref[8 * n : 8 * n + 8, :],
            ]
        )

    item = lane % 64
    end_lane = jnp.where(item < 16, item + (W - 16), jnp.where(item < 32, item - 16, 0))
    side_lane = jnp.clip(jnp.where(item < 48, (item - 33) * 16 + 15, (item - 49) * 16), 0, W - 1)
    corner_lane = jnp.where(item < 40, W - 1, jnp.where(item < 45, 15, jnp.where(item < 52, W - 16, 0)))
    is_corner = (item == 32) | (item == 41) | (item == 48) | (item == 57)

    def picked(values, index):
        return jnp.take_along_axis(values, index, axis=1)

    for r in range(3):
        send_ref[pl.ds(r, 8, stride=3), :] = zero
    coarse = part(0)
    for n in range(1, 8):
        north, south = along_columns(coarse)
        image = []
        for b in range(4):
            east, west = along_rows(coarse[b], *neighbours(coarse[b]))
            slope = along_x * (east - west) + along_y * (north[b] - south[b])
            total = (east + west) + (north[b] + south[b])
            image.append(coarse[b] + (spread * (total - 4.0 * coarse[b]) - coarse[b] * slope))
        image = cleared(image)
        beside = [neighbours(tile) for tile in image]

        rows = []
        for b in (1, 2):
            ends = picked(jnp.where(lane >= 64, beside[b][1], beside[b][0]), end_lane)
            sides = picked(jnp.where(column == 15, image[b - 1], image[b + 1]), side_lane)
            corners = jnp.where(
                lane >= 64,
                jnp.where(column == 15, beside[b - 1][1], beside[b + 1][1]),
                jnp.where(column == 15, beside[b - 1][0], beside[b + 1][0]),
            )
            corners = picked(corners, corner_lane)
            rows.append(jnp.where(item < 32, ends, jnp.where(is_corner, corners, sides)))
        base = n * 24
        send_ref[pl.ds(base, 8, stride=3), :] = image[1]
        send_ref[pl.ds(base + 1, 8, stride=3), :] = image[2]
        send_ref[pl.ds(base + 2, 8, stride=3), :] = jnp.where(lane < 64, rows[0], rows[1])

        if n < 7:
            blended = []
            for tile, pair in zip(image, beside):
                east, west = along_rows(tile, *pair)
                blended.append(BLEND[0] * west + BLEND[1] * tile + BLEND[2] * east)
            north, south = along_columns(blended)
            coarse = cleared(
                [
                    value + (BLEND[0] * s + BLEND[1] * tile + BLEND[2] * n_)
                    for value, s, tile, n_ in zip(part(n), south, blended, north)
                ]
            )


def base_kernel(end_ref, change_ref, base_ref, along_ref, fine_ref):
    lo = low(HALF)
    for j in range(CX):
        lower = change_ref[j * OROWS : (j + 1) * OROWS, :]
        middle = change_ref[(j + 1) * OROWS : (j + 2) * OROWS, :]
        upper = change_ref[(j + 2) * OROWS : (j + 3) * OROWS, :]
        for offset in range(4):
            along = WEIGHTS_MID[offset] * middle
            if offset < 2:
                along = along + WEIGHTS_LOW[offset] * lower
            else:
                along = along + WEIGHTS_HIGH[offset] * upper
            slot = offset * OROWS
            along_ref[slot : slot + OROWS, :] = along
            before = along_ref[slot : slot + CY, :]
            centre = along_ref[slot + 1 : slot + CY + 1, :]
            after = along_ref[slot + 2 : slot + CY + 2, :]
            for k in range(4):
                value = WEIGHTS_MID[k] * centre
                if k < 2:
                    value = value + WEIGHTS_LOW[k] * before
                else:
                    value = value + WEIGHTS_HIGH[k] * after
                fine_ref[pl.ds(offset * HALF + k, CY, stride=4), :] = value
        for pair in range(2):
            x = 4 * j + 2 * pair
            one = end_ref[x * HALF : (x + 1) * HALF, :] + fine_ref[2 * pair * HALF : (2 * pair + 1) * HALF, :]
            two = (
                end_ref[(x + 1) * HALF : (x + 2) * HALF, :]
                + fine_ref[(2 * pair + 1) * HALF : (2 * pair + 2) * HALF, :]
            )
            both = jnp.concatenate([jnp.where(lo, one, swap(two)), jnp.where(lo, swap(one), two)], axis=0).T
            base_ref[x * LEVELS : (x + 2) * LEVELS, :] = both


def column_weights():
    weights = np.zeros((3 * W, 10, W), np.float32)

    def put(k, j, cy):
        for offset in range(4):
            for at, factor in ((4 * (cy + 1), WEIGHTS_LOW), (4 * cy, WEIGHTS_MID), (4 * (cy - 1), WEIGHTS_HIGH)):
                if 0 <= at + offset < W:
                    weights[k, j, at + offset] += factor[offset]

    for h in range(2):
        for cx in range(CX):
            for c in range(CY):
                put(h * W + cx * CY + c, cx + 1, h * CY + c)
        for c in range(CY):
            put(2 * W + h * 64 + c, 0, h * CY + c)
            put(2 * W + h * 64 + CY + c, 9, h * CY + c)
        for j in range(10):
            if h == 0:
                put(2 * W + 32 + j, j, -1)
            else:
                put(2 * W + 64 + 48 + j, j, 2 * CY)
    return weights.reshape(3 * W, 10 * W).astype(ml_dtypes.bfloat16)


def end_kernel(base_ref, back_ref, weights_ref, out_ref, stage_ref, sem):
    values = jnp.concatenate([back_ref[pl.ds(r, LEVELS, stride=3), :] for r in range(3)], axis=1)
    first = values.astype(jnp.bfloat16)
    rest = values - first.astype(F32)
    second = rest.astype(jnp.bfloat16)
    third = (rest - second.astype(F32)).astype(jnp.bfloat16)
    stacked = jnp.concatenate([first, second, third], axis=0)
    columns = []
    copies = []
    for pair in range(5):
        product = jnp.dot(
            stacked, weights_ref[:, 2 * pair * W : 2 * (pair + 1) * W], preferred_element_type=F32
        )
        product = product[:LEVELS] + (product[LEVELS : 2 * LEVELS] + product[2 * LEVELS :])
        columns += [product[:, :W], product[:, W:]]
        if pair == 0:
            continue
        block = pair - 1
        for j in range(2 * block, 2 * block + 2):
            for offset in range(4):
                value = WEIGHTS_MID[offset] * columns[j + 1]
                if offset < 2:
                    value = value + WEIGHTS_LOW[offset] * columns[j]
                else:
                    value = value + WEIGHTS_HIGH[offset] * columns[j + 2]
                x = 4 * j + offset
                stage_ref[pl.ds(block * 8 * LEVELS + x % 8, LEVELS, stride=8), :] = (
                    base_ref[x * LEVELS : (x + 1) * LEVELS, :] + value
                )
        copy = pltpu.make_async_copy(
            stage_ref.reshape(4, LEVELS, 8, W).at[block], out_ref.at[:, pl.ds(8 * block, 8), :], sem.at[block]
        )
        copy.start()
        copies.append(copy)
    for copy in copies:
        copy.wait()


def shape(rows):
    return jax.ShapeDtypeStruct((rows, W), F32)


VMEM = pl.BlockSpec(memory_space=pltpu.VMEM)
SMEM = pl.BlockSpec(memory_space=pltpu.SMEM)
HBM = pl.BlockSpec(memory_space=pltpu.HBM)


def scratch(rows):
    return pltpu.VMEM((rows, W), F32)


def call(kernel, out_shape, in_specs, scratch_shapes, name, aliases=None, out_specs=None, cost=None, limit=24):
    many = isinstance(out_shape, tuple)
    return pl.pallas_call(
        kernel,
        out_shape=out_shape,
        in_specs=in_specs,
        out_specs=out_specs or ((VMEM,) * len(out_shape) if many else VMEM),
        scratch_shapes=scratch_shapes,
        input_output_aliases=aliases or {},
        cost_estimate=cost,
        compiler_params=pltpu.CompilerParams(vmem_limit_bytes=limit * 1024 * 1024),
        name=name,
    )


def ring(array, axis, distance):
    devices = lax.axis_size(axis)
    return lax.ppermute(array, axis, [(i, (i + distance) % devices) for i in range(devices)])


def shards(state_starts, diffusivity, wind):
    place = jnp.stack([lax.axis_index(axis) for axis in ("tm", "gx", "gy")]).astype(jnp.int32)
    field = state_starts.reshape(LEVELS, NX, W)
    edges, first_rows, last_rows = call(
        edge_kernel,
        (shape(16 * HALF), shape(STRIP), shape(STRIP)),
        [VMEM] * 2,
        [scratch(HALF)],
        "edges",
    )(field[:, :8].reshape(8 * LEVELS, W), field[:, NX - 8 :].reshape(8 * LEVELS, W))
    west = ring(last_rows, "gx", 1)
    east = ring(first_rows, "gx", -1)
    middle = call(
        middle_kernel,
        shape(16 * HALF),
        [VMEM],
        [],
        "middle",
        cost=pl.CostEstimate(flops=1 << 20, bytes_accessed=1 << 20, transcendentals=0),
    )(field[:, 8 : NX - 8].reshape(16 * LEVELS, W))
    first_columns, last_columns = call(side_kernel, (shape(SIDE), shape(SIDE)), [VMEM] * 4, [], "sides")(
        edges, middle, west, east
    )
    left = ring(last_columns, "gy", 1)
    right = ring(first_columns, "gy", -1)
    diffuse_row = diffusivity.reshape(1, LEVELS)
    states = (shape(40 * FROWS),) * 4 + (shape(NX * HALF), shape(12 * CROWS))
    inner = call(
        inner_kernel,
        states,
        [SMEM] + [VMEM] * 6,
        [scratch(FROWS)],
        "inner",
        cost=pl.CostEstimate(flops=1 << 24, bytes_accessed=8 << 20, transcendentals=0),
    )(place, edges, middle, west, east, diffuse_row, wind)
    outer = call(
        outer_kernel,
        states + (shape(10 * OROWS), shape(2 * LEVELS)),
        [SMEM] + [VMEM] * 12,
        [scratch(160 + CX * HALF), scratch(CX * OROWS), scratch(W)],
        "outer",
        aliases={7 + k: k for k in range(6)},
    )(place, west, east, left, right, diffuse_row, wind, *inner)
    fine_end, change, parts = outer[4], outer[6], outer[7]
    parts = lax.all_to_all(parts.reshape(LEVELS, 2, W), ("tm", "gx"), 0, 0, tiled=True).reshape(2 * LEVELS, W)
    first_half, second_half = call(split_kernel, (shape(LEVELS), shape(LEVELS)), [VMEM], [], "split")(parts)
    left = ring(second_half, "gy", 1)
    right = ring(first_half, "gy", -1)
    parts, fine_end = lax.optimization_barrier((parts, fine_end))
    base = call(
        base_kernel,
        shape(NX * LEVELS),
        [VMEM] * 2,
        [scratch(4 * OROWS), scratch(4 * HALF)],
        "base",
        cost=pl.CostEstimate(flops=1 << 22, bytes_accessed=2 << 20, transcendentals=0),
    )(fine_end, change)
    left, right, base = lax.optimization_barrier((left, right, base))
    images = call(chain_kernel, shape(3 * LEVELS), [SMEM] * 3 + [VMEM] * 3, [], "chain")(
        place, diffusivity, wind, parts, left, right
    )
    images = lax.all_to_all(images.reshape(LEVELS, 1, 3 * W), ("tm", "gx"), 0, 0, tiled=True)
    ending = call(
        end_kernel,
        jax.ShapeDtypeStruct((LEVELS, NX, W), F32),
        [VMEM] * 3,
        [scratch(NX * LEVELS), pltpu.SemaphoreType.DMA((4,))],
        "ending",
        out_specs=HBM,
    )(base, images.reshape(3 * LEVELS, W), jnp.asarray(column_weights()))
    return ending.reshape(1, LEVELS, NX, W)


def solution(mesh):
    placed = (P("tm", None, "gx", "gy"), P(), P())
    return jax.shard_map(
        shards, mesh=mesh, in_specs=placed, out_specs=P("tm", None, "gx", "gy"), check_vma=False
    )
```

```python
import jax
import jax.numpy as jnp
import ml_dtypes
import numpy as np
from jax import lax
from jax.experimental import pallas as pl
from jax.experimental.pallas import tpu as pltpu
from jax.sharding import PartitionSpec as P

SUB = 4
STEP = 0.2
LEVELS = 64
NX = 32
HALF = 64
CX = NX // 4
CY = HALF // 4
W = 128
WEIGHTS_LOW = (0.375, 0.125, 0.0, 0.0)
WEIGHTS_MID = (0.625, 0.875, 0.875, 0.625)
WEIGHTS_HIGH = (0.0, 0.0, 0.125, 0.375)
BLEND = (0.125, 0.75, 0.125)
F32 = jnp.float32

STRIP = 4 * HALF + CY
SIDE = 20 * 8 + 8
FROWS = 88
CROWS = 40
OROWS = 24


def lanes(rows):
    return lax.broadcasted_iota(jnp.int32, (rows, W), 1)


def rows_of(rows):
    return lax.broadcasted_iota(jnp.int32, (rows, W), 0)


def low(rows):
    return lanes(rows) < LEVELS


def swap(value):
    return pltpu.roll(value, LEVELS, 1)


def coarse_rows(ref, start, count):
    total = ref[pl.ds(start, count, stride=4), :]
    for offset in range(1, 4):
        total = total + ref[pl.ds(start + offset, count, stride=4), :]
    return total * (1.0 / 16.0)


def turned_pair(rows_ref, x, stride):
    lo = low(HALF)
    both = jnp.concatenate(
        [rows_ref[pl.ds(x, LEVELS, stride=stride), :], rows_ref[pl.ds(x + 1, LEVELS, stride=stride), :]], axis=0
    ).T
    top = both[:HALF]
    bottom = both[HALF:]
    return jnp.where(lo, top, swap(bottom)), jnp.where(lo, swap(top), bottom)


def edge_kernel(low_ref, high_ref, edge_ref, first_ref, last_ref, sum_ref):
    for side, (rows_ref, strip_ref) in enumerate(((low_ref, first_ref), (high_ref, last_ref))):
        rows = []
        for x in range(0, 8, 2):
            rows += turned_pair(rows_ref, x, 8)
        for x in range(8):
            base = (8 * side + x) * HALF
            edge_ref[base : base + HALF, :] = rows[x]
        near = rows[:4] if side == 0 else rows[4:]
        far = rows[4:] if side == 0 else rows[:4]
        for x in range(4):
            strip_ref[x * HALF : (x + 1) * HALF, :] = near[x]
        sum_ref[...] = (far[0] + far[1]) + (far[2] + far[3])
        strip_ref[4 * HALF :, :] = coarse_rows(sum_ref, 0, CY)


def middle_kernel(rows_ref, middle_ref):
    for x in range(0, 16, 2):
        one, two = turned_pair(rows_ref, x, 16)
        middle_ref[x * HALF : (x + 1) * HALF, :] = one
        middle_ref[(x + 1) * HALF : (x + 2) * HALF, :] = two


def block_row(x, edge_ref, middle_ref, west_ref, east_ref):
    if x < 0:
        return west_ref, (x + 4) * HALF
    if x >= NX:
        return east_ref, (x - NX) * HALF
    if x < 8:
        return edge_ref, x * HALF
    if x >= NX - 8:
        return edge_ref, (x - NX + 16) * HALF
    return middle_ref, (x - 8) * HALF


def side_kernel(edge_ref, middle_ref, west_ref, east_ref, left_ref, right_ref):
    lo = low(8)

    def edge(x, start):
        source, base = block_row(x, edge_ref, middle_ref, west_ref, east_ref)
        return source[base + start : base + start + 8, :]

    for i in range(20):
        left_ref[8 * i : 8 * i + 8, :] = jnp.where(lo, edge(i - 4, 0), swap(edge(i + 16, 0)))
        right_ref[8 * i : 8 * i + 8, :] = jnp.where(
            lo, swap(edge(i - 4, HALF - 8)), edge(i + 16, HALF - 8)
        )
    base = 4 * HALF
    left_ref[160:168, :] = jnp.where(lo, west_ref[base : base + 8, :], swap(east_ref[base : base + 8, :]))
    right_ref[160:168, :] = jnp.where(
        lo, swap(west_ref[base + 8 : base + 16, :]), east_ref[base + 8 : base + 16, :]
    )


def both_halves(values):
    return jnp.concatenate([values, values], axis=1)


def coefficients(diffuse_ref, wind_ref):
    diffuse = both_halves(diffuse_ref[...])
    wind = both_halves(wind_ref[...])
    spread = jnp.broadcast_to(STEP * diffuse, (8, W))
    along_x = jnp.broadcast_to((0.5 * STEP) * wind[0:1], (8, W))
    along_y = jnp.broadcast_to((0.5 * STEP) * wind[1:2], (8, W))
    return spread, along_x, along_y


def advanced(ref, r, rows, coefs, factor):
    spread, along_x, along_y = coefs
    centre = ref[r : r + 8, :]
    east = ref[r + rows : r + rows + 8, :]
    west = ref[r - rows : r - rows + 8, :]
    north = ref[r + 1 : r + 9, :]
    south = ref[r - 1 : r + 7, :]
    slope = along_x * (east - west) + along_y * (north - south)
    return centre + ((factor * spread) * ((east + west) + (north + south) - 4.0 * centre) - centre * slope)


def substeps(states, end_ref, coefs, tiles, end_tiles):
    at_west = lax.axis_index("gx") == 0
    at_east = lax.axis_index("gx") == 7
    lo = low(8)
    zero8 = jnp.zeros((8, W), F32)
    left_out = jnp.logical_and(lax.axis_index("gy") == 0, jnp.logical_and(rows_of(8) < 4, lo))
    right_out = jnp.logical_and(lax.axis_index("gy") == 3, jnp.logical_and(rows_of(8) >= 4, jnp.logical_not(lo)))
    for step in range(SUB - 1):
        for tile in tiles:
            for i in range(step + 1, 39 - step):
                r = i * FROWS + 8 + 8 * tile
                value = advanced(states[step], r, FROWS, coefs, 1.0)
                if tile == 0:
                    value = jnp.where(left_out, zero8, value)
                if tile == 8:
                    value = jnp.where(right_out, zero8, value)
                if i < 4:
                    value = jnp.where(at_west, zero8, value)
                if i >= 36:
                    value = jnp.where(at_east, zero8, value)
                states[step + 1][r : r + 8, :] = value
    for tile in end_tiles:
        for i in range(4, 36):
            o = (i - 4) * HALF + 8 * tile
            end_ref[o : o + 8, :] = advanced(states[SUB - 1], i * FROWS + 12 + 8 * tile, FROWS, coefs, 1.0)


def inner_kernel(
    edge_ref, middle_ref, west_ref, east_ref, diffuse_ref, wind_ref,
    s0_ref, s1_ref, s2_ref, s3_ref, end_ref, coarse_ref, sum_ref,
):
    lo8 = low(8)
    zero8 = jnp.zeros((8, W), F32)
    for i in range(40):
        source, base = block_row(i - 4, edge_ref, middle_ref, west_ref, east_ref)
        rows = source[base : base + HALF, :]
        before = jnp.where(lo8, zero8, swap(rows[HALF - 8 :]))
        after = jnp.where(lo8, swap(rows[:8]), zero8)
        if i < 4 or i >= 36:
            outside = lax.axis_index("gx") == (0 if i < 4 else 7)
            rows = jnp.where(outside, jnp.zeros_like(rows), rows)
            before = jnp.where(outside, zero8, before)
            after = jnp.where(outside, zero8, after)
        start = i * FROWS
        s0_ref[start : start + 4, :] = zero8[:4]
        s0_ref[start + 4 : start + 12, :] = before
        s0_ref[start + 12 : start + 76, :] = rows
        s0_ref[start + 76 : start + 84, :] = after
        s0_ref[start + 84 : start + 88, :] = zero8[:4]

    coarse_ref[...] = jnp.zeros_like(coarse_ref)
    for j in range(10):
        base = 4 * j * FROWS
        sum_ref[...] = (s0_ref[base : base + FROWS, :] + s0_ref[base + FROWS : base + 2 * FROWS, :]) + (
            s0_ref[base + 2 * FROWS : base + 3 * FROWS, :] + s0_ref[base + 3 * FROWS : base + 4 * FROWS, :]
        )
        start = (j + 1) * CROWS
        coarse_ref[start + 7 : start + 27, :] = coarse_rows(sum_ref, 4, 20)

    states = (s0_ref, s1_ref, s2_ref, s3_ref)
    substeps(states, end_ref, coefficients(diffuse_ref, wind_ref), range(9), range(8))


def outer_kernel(
    west_ref, east_ref, left_ref, right_ref, diffuse_ref, wind_ref,
    s0_in, s1_in, s2_in, s3_in, end_in, coarse_in,
    s0_ref, s1_ref, s2_ref, s3_ref, end_ref, coarse_ref, change_ref, send_ref,
    sum_ref, blend_ref, part_ref,
):
    del s0_in, s1_in, s2_in, s3_in, end_in, coarse_in
    first_segment = lax.axis_index("tm") == 0
    at_west = lax.axis_index("gx") == 0
    at_east = lax.axis_index("gx") == 7
    at_left = lax.axis_index("gy") == 0
    at_right = lax.axis_index("gy") == 3
    lo8 = low(8)
    zero8 = jnp.zeros((8, W), F32)
    coefs = coefficients(diffuse_ref, wind_ref)

    for j in range(10):
        befores = []
        afters = []
        for i in range(4 * j, 4 * j + 4):
            k = i % 20
            from_left = left_ref[8 * k : 8 * k + 8, :]
            from_right = right_ref[8 * k : 8 * k + 8, :]
            if i >= 20:
                from_left = swap(from_left)
            else:
                from_right = swap(from_right)
            start = i * FROWS
            known = s0_ref[start + 4 : start + 12, :]
            before = jnp.where(lo8, jnp.where(at_left, zero8, from_left), known)
            known = s0_ref[start + 76 : start + 84, :]
            after = jnp.where(lo8, known, jnp.where(at_right, zero8, from_right))
            if i < 4 or i >= 36:
                outside = at_west if i < 4 else at_east
                before = jnp.where(outside, zero8, before)
                after = jnp.where(outside, zero8, after)
            s0_ref[start + 4 : start + 12, :] = before
            s0_ref[start + 76 : start + 84, :] = after
            befores.append(before)
            afters.append(after)
        base = 16 * j
        sum_ref[base : base + 8, :] = (befores[0] + befores[1]) + (befores[2] + befores[3])
        sum_ref[base + 8 : base + 16, :] = (afters[0] + afters[1]) + (afters[2] + afters[3])
        start = (j + 1) * CROWS
        coarse_ref[start + 7 : start + 9, :] = coarse_rows(sum_ref, base, 2)
        coarse_ref[start + 25 : start + 27, :] = coarse_rows(sum_ref, base + 8, 2)
    left_corner = left_ref[160:168, :]
    right_corner = right_ref[160:168, :]
    for source, start, outside, is_west in (
        (west_ref, 0, at_west, True),
        (east_ref, 11 * CROWS, at_east, False),
    ):
        rows = source[4 * HALF :, :]
        from_left = left_corner if is_west else swap(left_corner)
        from_right = swap(right_corner) if is_west else right_corner
        from_left = jnp.where(at_left, zero8, from_left)
        from_right = jnp.where(at_right, zero8, from_right)
        before = jnp.where(lo8, from_left, swap(rows[8:]))
        after = jnp.where(lo8, swap(rows[:8]), from_right)
        coarse_ref[start + 1 : start + 9, :] = jnp.where(outside, zero8, before)
        coarse_ref[start + 9 : start + 25, :] = jnp.where(outside, jnp.zeros_like(rows), rows)
        coarse_ref[start + 25 : start + 33, :] = jnp.where(outside, zero8, after)

    for j in range(10):
        for tile in range(3):
            image = advanced(coarse_ref, (j + 1) * CROWS + 8 + 8 * tile, CROWS, coefs, 0.25)
            cy = rows_of(8) + (8 * tile - 1)
            outside = cy > CY
            if tile == 0:
                outside = jnp.logical_or(outside, jnp.logical_and(at_left, jnp.logical_and(cy < 0, lo8)))
            if tile == 2:
                outside = jnp.logical_or(
                    outside, jnp.logical_and(at_right, jnp.logical_and(cy >= CY, jnp.logical_not(lo8)))
                )
            if j == 0:
                outside = jnp.logical_or(outside, at_west)
            if j == 9:
                outside = jnp.logical_or(outside, at_east)
            image = jnp.where(outside, zero8, image)
            o = j * OROWS + 8 * tile
            change_ref[o : o + 8, :] = jnp.where(first_segment, image, zero8) - image

    states = (s0_ref, s1_ref, s2_ref, s3_ref)
    substeps(states, end_ref, coefs, (0, 8), (0, 7))

    for j in range(CX):
        lower = change_ref[j * OROWS : (j + 1) * OROWS, :]
        middle = change_ref[(j + 1) * OROWS : (j + 2) * OROWS, :]
        upper = change_ref[(j + 2) * OROWS : (j + 3) * OROWS, :]
        slot = j * OROWS
        blend_ref[slot : slot + OROWS, :] = BLEND[0] * lower + BLEND[1] * middle + BLEND[2] * upper
        blended = (
            BLEND[0] * blend_ref[slot : slot + CY, :]
            + BLEND[1] * blend_ref[slot + 1 : slot + CY + 1, :]
            + BLEND[2] * blend_ref[slot + 2 : slot + CY + 2, :]
        )
        base = 4 * j * HALF
        total = (end_ref[base : base + HALF, :] + end_ref[base + HALF : base + 2 * HALF, :]) + (
            end_ref[base + 2 * HALF : base + 3 * HALF, :] + end_ref[base + 3 * HALF : base + 4 * HALF, :]
        )
        spot = 160 + j * HALF
        sum_ref[spot : spot + HALF, :] = total
        part_ref[j * CY : (j + 1) * CY, :] = coarse_rows(sum_ref, spot, CY) + blended
    turned = part_ref[...].T
    for h in range(2):
        send_ref[pl.ds(h, LEVELS, stride=2), :] = turned[h * LEVELS : (h + 1) * LEVELS]


def split_kernel(part_ref, first_ref, second_ref):
    first_ref[...] = part_ref[pl.ds(0, LEVELS, stride=2), :]
    second_ref[...] = part_ref[pl.ds(1, LEVELS, stride=2), :]


def chain_kernel(level_ref, part_ref, left_ref, right_ref, send_ref):
    at_left = lax.axis_index("gy") == 0
    at_right = lax.axis_index("gy") == 3
    spread = (0.25 * STEP) * level_ref[0:8, :]
    along_x = (0.5 * STEP) * level_ref[8:16, :]
    along_y = (0.5 * STEP) * level_ref[16:24, :]

    lane = lanes(8)
    row = rows_of(8)
    column = lane % 16
    zero = jnp.zeros((8, W), F32)

    def neighbours(tile):
        up = jnp.where(row < 7, pltpu.roll(tile, 7, 0), zero)
        down = jnp.where(row > 0, pltpu.roll(tile, 1, 0), zero)
        return up, down

    def along_rows(tile, up, down):
        east = pltpu.roll(jnp.where(lane < 16, up, tile), W - 16, 1)
        west = pltpu.roll(jnp.where(lane >= W - 16, down, tile), 16, 1)
        return east, west

    def along_columns(tiles):
        after = [pltpu.roll(tile, W - 1, 1) for tile in tiles]
        before = [pltpu.roll(tile, 1, 1) for tile in tiles]
        after_far = [pltpu.roll(tile, 15, 1) for tile in tiles[1:]] + [zero]
        before_far = [zero] + [pltpu.roll(tile, W - 15, 1) for tile in tiles[:-1]]
        north = [jnp.where(column < 15, near, far) for near, far in zip(after, after_far)]
        south = [jnp.where(column > 0, near, far) for near, far in zip(before, before_far)]
        return north, south

    def cleared(tiles):
        return [jnp.where(at_left, zero, tiles[0]), tiles[1], tiles[2], jnp.where(at_right, zero, tiles[3])]

    def part(n):
        return cleared(
            [
                left_ref[8 * n : 8 * n + 8, :],
                part_ref[pl.ds(16 * n, 8, stride=2), :],
                part_ref[pl.ds(16 * n + 1, 8, stride=2), :],
                right_ref[8 * n : 8 * n + 8, :],
            ]
        )

    item = lane % 64
    end_lane = jnp.where(item < 16, item + (W - 16), jnp.where(item < 32, item - 16, 0))
    side_lane = jnp.clip(jnp.where(item < 48, (item - 33) * 16 + 15, (item - 49) * 16), 0, W - 1)
    corner_lane = jnp.where(item < 40, W - 1, jnp.where(item < 45, 15, jnp.where(item < 52, W - 16, 0)))
    is_corner = (item == 32) | (item == 41) | (item == 48) | (item == 57)

    def picked(values, index):
        return jnp.take_along_axis(values, index, axis=1)

    for r in range(3):
        send_ref[pl.ds(r, 8, stride=3), :] = zero
    coarse = part(0)
    for n in range(1, 8):
        north, south = along_columns(coarse)
        image = []
        for b in range(4):
            east, west = along_rows(coarse[b], *neighbours(coarse[b]))
            slope = along_x * (east - west) + along_y * (north[b] - south[b])
            total = (east + west) + (north[b] + south[b])
            image.append(coarse[b] + (spread * (total - 4.0 * coarse[b]) - coarse[b] * slope))
        image = cleared(image)
        beside = [neighbours(tile) for tile in image]

        rows = []
        for b in (1, 2):
            ends = picked(jnp.where(lane >= 64, beside[b][1], beside[b][0]), end_lane)
            sides = picked(jnp.where(column == 15, image[b - 1], image[b + 1]), side_lane)
            corners = jnp.where(
                lane >= 64,
                jnp.where(column == 15, beside[b - 1][1], beside[b + 1][1]),
                jnp.where(column == 15, beside[b - 1][0], beside[b + 1][0]),
            )
            corners = picked(corners, corner_lane)
            rows.append(jnp.where(item < 32, ends, jnp.where(is_corner, corners, sides)))
        base = n * 24
        send_ref[pl.ds(base, 8, stride=3), :] = image[1]
        send_ref[pl.ds(base + 1, 8, stride=3), :] = image[2]
        send_ref[pl.ds(base + 2, 8, stride=3), :] = jnp.where(lane < 64, rows[0], rows[1])

        if n < 7:
            blended = []
            for tile, pair in zip(image, beside):
                east, west = along_rows(tile, *pair)
                blended.append(BLEND[0] * west + BLEND[1] * tile + BLEND[2] * east)
            north, south = along_columns(blended)
            coarse = cleared(
                [
                    value + (BLEND[0] * s + BLEND[1] * tile + BLEND[2] * n_)
                    for value, s, tile, n_ in zip(part(n), south, blended, north)
                ]
            )


def base_kernel(end_ref, change_ref, base_ref, along_ref, fine_ref):
    lo = low(HALF)
    for j in range(CX):
        lower = change_ref[j * OROWS : (j + 1) * OROWS, :]
        middle = change_ref[(j + 1) * OROWS : (j + 2) * OROWS, :]
        upper = change_ref[(j + 2) * OROWS : (j + 3) * OROWS, :]
        for offset in range(4):
            along = WEIGHTS_MID[offset] * middle
            if offset < 2:
                along = along + WEIGHTS_LOW[offset] * lower
            else:
                along = along + WEIGHTS_HIGH[offset] * upper
            slot = offset * OROWS
            along_ref[slot : slot + OROWS, :] = along
            before = along_ref[slot : slot + CY, :]
            centre = along_ref[slot + 1 : slot + CY + 1, :]
            after = along_ref[slot + 2 : slot + CY + 2, :]
            for k in range(4):
                value = WEIGHTS_MID[k] * centre
                if k < 2:
                    value = value + WEIGHTS_LOW[k] * before
                else:
                    value = value + WEIGHTS_HIGH[k] * after
                fine_ref[pl.ds(offset * HALF + k, CY, stride=4), :] = value
        for pair in range(2):
            x = 4 * j + 2 * pair
            one = end_ref[x * HALF : (x + 1) * HALF, :] + fine_ref[2 * pair * HALF : (2 * pair + 1) * HALF, :]
            two = (
                end_ref[(x + 1) * HALF : (x + 2) * HALF, :]
                + fine_ref[(2 * pair + 1) * HALF : (2 * pair + 2) * HALF, :]
            )
            both = jnp.concatenate([jnp.where(lo, one, swap(two)), jnp.where(lo, swap(one), two)], axis=0).T
            base_ref[x * LEVELS : (x + 2) * LEVELS, :] = both


def column_weights():
    weights = np.zeros((3 * W, 10, W), np.float32)

    def put(k, j, cy):
        for offset in range(4):
            for at, factor in ((4 * (cy + 1), WEIGHTS_LOW), (4 * cy, WEIGHTS_MID), (4 * (cy - 1), WEIGHTS_HIGH)):
                if 0 <= at + offset < W:
                    weights[k, j, at + offset] += factor[offset]

    for h in range(2):
        for cx in range(CX):
            for c in range(CY):
                put(h * W + cx * CY + c, cx + 1, h * CY + c)
        for c in range(CY):
            put(2 * W + h * 64 + c, 0, h * CY + c)
            put(2 * W + h * 64 + CY + c, 9, h * CY + c)
        for j in range(10):
            if h == 0:
                put(2 * W + 32 + j, j, -1)
            else:
                put(2 * W + 64 + 48 + j, j, 2 * CY)
    return weights.reshape(3 * W, 10 * W).astype(ml_dtypes.bfloat16)


def end_kernel(base_ref, back_ref, weights_ref, out_ref, stage_ref, sem):
    values = jnp.concatenate([back_ref[pl.ds(r, LEVELS, stride=3), :] for r in range(3)], axis=1)
    first = values.astype(jnp.bfloat16)
    rest = values - first.astype(F32)
    second = rest.astype(jnp.bfloat16)
    third = (rest - second.astype(F32)).astype(jnp.bfloat16)
    stacked = jnp.concatenate([first, second, third], axis=0)
    columns = []
    copies = []
    for pair in range(5):
        product = jnp.dot(
            stacked, weights_ref[:, 2 * pair * W : 2 * (pair + 1) * W], preferred_element_type=F32
        )
        product = product[:LEVELS] + (product[LEVELS : 2 * LEVELS] + product[2 * LEVELS :])
        columns += [product[:, :W], product[:, W:]]
        if pair == 0:
            continue
        block = pair - 1
        for j in range(2 * block, 2 * block + 2):
            for offset in range(4):
                value = WEIGHTS_MID[offset] * columns[j + 1]
                if offset < 2:
                    value = value + WEIGHTS_LOW[offset] * columns[j]
                else:
                    value = value + WEIGHTS_HIGH[offset] * columns[j + 2]
                x = 4 * j + offset
                stage_ref[pl.ds(block * 8 * LEVELS + x % 8, LEVELS, stride=8), :] = (
                    base_ref[x * LEVELS : (x + 1) * LEVELS, :] + value
                )
        copy = pltpu.make_async_copy(
            stage_ref.reshape(4, LEVELS, 8, W).at[block], out_ref.at[:, pl.ds(8 * block, 8), :], sem.at[block]
        )
        copy.start()
        copies.append(copy)
    for copy in copies:
        copy.wait()


def shape(rows):
    return jax.ShapeDtypeStruct((rows, W), F32)


VMEM = pl.BlockSpec(memory_space=pltpu.VMEM)
HBM = pl.BlockSpec(memory_space=pltpu.HBM)


def scratch(rows):
    return pltpu.VMEM((rows, W), F32)


def call(kernel, out_shape, in_specs, scratch_shapes, name, aliases=None, out_specs=None, cost=None, limit=24):
    many = isinstance(out_shape, tuple)
    return pl.pallas_call(
        kernel,
        out_shape=out_shape,
        in_specs=in_specs,
        out_specs=out_specs or ((VMEM,) * len(out_shape) if many else VMEM),
        scratch_shapes=scratch_shapes,
        input_output_aliases=aliases or {},
        cost_estimate=cost,
        compiler_params=pltpu.CompilerParams(vmem_limit_bytes=limit * 1024 * 1024),
        name=name,
    )


def ring(array, axis, distance):
    devices = lax.axis_size(axis)
    return lax.ppermute(array, axis, [(i, (i + distance) % devices) for i in range(devices)])


def shards(state_starts, diffusivity, wind):
    field = state_starts.reshape(LEVELS, NX, W)
    edges, first_rows, last_rows = call(
        edge_kernel,
        (shape(16 * HALF), shape(STRIP), shape(STRIP)),
        [VMEM] * 2,
        [scratch(HALF)],
        "edges",
    )(field[:, :8].reshape(8 * LEVELS, W), field[:, NX - 8 :].reshape(8 * LEVELS, W))
    west = ring(last_rows, "gx", 1)
    east = ring(first_rows, "gx", -1)
    middle = call(
        middle_kernel,
        shape(16 * HALF),
        [VMEM],
        [],
        "middle",
        cost=pl.CostEstimate(flops=1 << 20, bytes_accessed=1 << 20, transcendentals=0),
    )(field[:, 8 : NX - 8].reshape(16 * LEVELS, W))
    first_columns, last_columns = call(side_kernel, (shape(SIDE), shape(SIDE)), [VMEM] * 4, [], "sides")(
        edges, middle, west, east
    )
    left = ring(last_columns, "gy", 1)
    right = ring(first_columns, "gy", -1)
    level = lax.axis_index("tm") * 8 + lax.axis_index("gx")
    of_level = jnp.concatenate([diffusivity[None], wind], axis=0)
    of_level = lax.dynamic_slice_in_dim(of_level, level, 1, axis=1)
    of_level = jnp.broadcast_to(of_level[:, None, :], (3, 8, W)).reshape(24, W)
    diffuse_row = diffusivity.reshape(1, LEVELS)
    states = (shape(40 * FROWS),) * 4 + (shape(NX * HALF), shape(12 * CROWS))
    inner = call(
        inner_kernel,
        states,
        [VMEM] * 6,
        [scratch(FROWS)],
        "inner",
        cost=pl.CostEstimate(flops=1 << 24, bytes_accessed=8 << 20, transcendentals=0),
    )(edges, middle, west, east, diffuse_row, wind)
    outer = call(
        outer_kernel,
        states + (shape(10 * OROWS), shape(2 * LEVELS)),
        [VMEM] * 12,
        [scratch(160 + CX * HALF), scratch(CX * OROWS), scratch(W)],
        "outer",
        aliases={6 + k: k for k in range(6)},
    )(west, east, left, right, diffuse_row, wind, *inner)
    fine_end, change, parts = outer[4], outer[6], outer[7]
    parts = lax.all_to_all(parts.reshape(LEVELS, 2, W), ("tm", "gx"), 0, 0, tiled=True).reshape(2 * LEVELS, W)
    first_half, second_half = call(split_kernel, (shape(LEVELS), shape(LEVELS)), [VMEM], [], "split")(parts)
    left = ring(second_half, "gy", 1)
    right = ring(first_half, "gy", -1)
    parts, fine_end = lax.optimization_barrier((parts, fine_end))
    base = call(
        base_kernel,
        shape(NX * LEVELS),
        [VMEM] * 2,
        [scratch(4 * OROWS), scratch(4 * HALF)],
        "base",
        cost=pl.CostEstimate(flops=1 << 22, bytes_accessed=2 << 20, transcendentals=0),
    )(fine_end, change)
    left, right, base = lax.optimization_barrier((left, right, base))
    images = call(chain_kernel, shape(3 * LEVELS), [VMEM] * 4, [], "chain")(
        of_level, parts, left, right
    )
    images = lax.all_to_all(images.reshape(LEVELS, 1, 3 * W), ("tm", "gx"), 0, 0, tiled=True)
    ending = call(
        end_kernel,
        jax.ShapeDtypeStruct((LEVELS, NX, W), F32),
        [VMEM] * 3,
        [scratch(NX * LEVELS), pltpu.SemaphoreType.DMA((4,))],
        "ending",
        out_specs=HBM,
    )(base, images.reshape(3 * LEVELS, W), jnp.asarray(column_weights()))
    return ending.reshape(1, LEVELS, NX, W)


def solution(mesh):
    placed = (P("tm", None, "gx", "gy"), P(), P())
    return jax.shard_map(
        shards, mesh=mesh, in_specs=placed, out_specs=P("tm", None, "gx", "gy"), check_vma=False
    )
```

```python
import jax
import jax.numpy as jnp
import ml_dtypes
import numpy as np
from jax import lax
from jax.experimental import pallas as pl
from jax.experimental.pallas import tpu as pltpu
from jax.sharding import PartitionSpec as P

SUB = 4
STEP = 0.2
LEVELS = 64
NX = 32
HALF = 64
CX = NX // 4
CY = HALF // 4
W = 128
WEIGHTS_LOW = (0.375, 0.125, 0.0, 0.0)
WEIGHTS_MID = (0.625, 0.875, 0.875, 0.625)
WEIGHTS_HIGH = (0.0, 0.0, 0.125, 0.375)
BLEND = (0.125, 0.75, 0.125)
F32 = jnp.float32

STRIP = 4 * HALF + CY
SIDE = 20 * 8 + 8
FROWS = 88
CROWS = 40
OROWS = 24


def lanes(rows):
    return lax.broadcasted_iota(jnp.int32, (rows, W), 1)


def rows_of(rows):
    return lax.broadcasted_iota(jnp.int32, (rows, W), 0)


def low(rows):
    return lanes(rows) < LEVELS


def swap(value):
    return pltpu.roll(value, LEVELS, 1)


def coarse_rows(ref, start, count):
    total = ref[pl.ds(start, count, stride=4), :]
    for offset in range(1, 4):
        total = total + ref[pl.ds(start + offset, count, stride=4), :]
    return total * (1.0 / 16.0)


def turned_pair(rows_ref, x, stride):
    lo = low(HALF)
    both = jnp.concatenate(
        [rows_ref[pl.ds(x, LEVELS, stride=stride), :], rows_ref[pl.ds(x + 1, LEVELS, stride=stride), :]], axis=0
    ).T
    top = both[:HALF]
    bottom = both[HALF:]
    return jnp.where(lo, top, swap(bottom)), jnp.where(lo, swap(top), bottom)


def edge_kernel(low_ref, high_ref, edge_ref, first_ref, last_ref, sum_ref):
    for side, (rows_ref, strip_ref) in enumerate(((low_ref, first_ref), (high_ref, last_ref))):
        rows = []
        for x in range(0, 8, 2):
            rows += turned_pair(rows_ref, x, 8)
        for x in range(8):
            base = (8 * side + x) * HALF
            edge_ref[base : base + HALF, :] = rows[x]
        near = rows[:4] if side == 0 else rows[4:]
        far = rows[4:] if side == 0 else rows[:4]
        for x in range(4):
            strip_ref[x * HALF : (x + 1) * HALF, :] = near[x]
        sum_ref[...] = (far[0] + far[1]) + (far[2] + far[3])
        strip_ref[4 * HALF :, :] = coarse_rows(sum_ref, 0, CY)


def middle_kernel(rows_ref, middle_ref):
    for x in range(0, 16, 2):
        one, two = turned_pair(rows_ref, x, 16)
        middle_ref[x * HALF : (x + 1) * HALF, :] = one
        middle_ref[(x + 1) * HALF : (x + 2) * HALF, :] = two


def block_row(x, edge_ref, middle_ref, west_ref, east_ref):
    if x < 0:
        return west_ref, (x + 4) * HALF
    if x >= NX:
        return east_ref, (x - NX) * HALF
    if x < 8:
        return edge_ref, x * HALF
    if x >= NX - 8:
        return edge_ref, (x - NX + 16) * HALF
    return middle_ref, (x - 8) * HALF


def side_kernel(edge_ref, middle_ref, west_ref, east_ref, left_ref, right_ref):
    lo = low(8)

    def edge(x, start):
        source, base = block_row(x, edge_ref, middle_ref, west_ref, east_ref)
        return source[base + start : base + start + 8, :]

    for i in range(20):
        left_ref[8 * i : 8 * i + 8, :] = jnp.where(lo, edge(i - 4, 0), swap(edge(i + 16, 0)))
        right_ref[8 * i : 8 * i + 8, :] = jnp.where(
            lo, swap(edge(i - 4, HALF - 8)), edge(i + 16, HALF - 8)
        )
    base = 4 * HALF
    left_ref[160:168, :] = jnp.where(lo, west_ref[base : base + 8, :], swap(east_ref[base : base + 8, :]))
    right_ref[160:168, :] = jnp.where(
        lo, swap(west_ref[base + 8 : base + 16, :]), east_ref[base + 8 : base + 16, :]
    )


def both_halves(values):
    return jnp.concatenate([values, values], axis=1)


def coefficients(diffuse_ref, wind_ref):
    diffuse = both_halves(diffuse_ref[...])
    wind = both_halves(wind_ref[...])
    spread = jnp.broadcast_to(STEP * diffuse, (8, W))
    along_x = jnp.broadcast_to((0.5 * STEP) * wind[0:1], (8, W))
    along_y = jnp.broadcast_to((0.5 * STEP) * wind[1:2], (8, W))
    return spread, along_x, along_y


def advanced(ref, r, rows, coefs, factor):
    spread, along_x, along_y = coefs
    centre = ref[r : r + 8, :]
    east = ref[r + rows : r + rows + 8, :]
    west = ref[r - rows : r - rows + 8, :]
    north = ref[r + 1 : r + 9, :]
    south = ref[r - 1 : r + 7, :]
    slope = along_x * (east - west) + along_y * (north - south)
    return centre + ((factor * spread) * ((east + west) + (north + south) - 4.0 * centre) - centre * slope)


def substeps(states, end_ref, coefs, tiles, end_tiles):
    at_west = lax.axis_index("gx") == 0
    at_east = lax.axis_index("gx") == 7
    lo = low(8)
    zero8 = jnp.zeros((8, W), F32)
    left_out = jnp.logical_and(lax.axis_index("gy") == 0, jnp.logical_and(rows_of(8) < 4, lo))
    right_out = jnp.logical_and(lax.axis_index("gy") == 3, jnp.logical_and(rows_of(8) >= 4, jnp.logical_not(lo)))
    for step in range(SUB - 1):
        for tile in tiles:
            for i in range(step + 1, 39 - step):
                r = i * FROWS + 8 + 8 * tile
                value = advanced(states[step], r, FROWS, coefs, 1.0)
                if tile == 0:
                    value = jnp.where(left_out, zero8, value)
                if tile == 8:
                    value = jnp.where(right_out, zero8, value)
                if i < 4:
                    value = jnp.where(at_west, zero8, value)
                if i >= 36:
                    value = jnp.where(at_east, zero8, value)
                states[step + 1][r : r + 8, :] = value
    for tile in end_tiles:
        for i in range(4, 36):
            o = (i - 4) * HALF + 8 * tile
            end_ref[o : o + 8, :] = advanced(states[SUB - 1], i * FROWS + 12 + 8 * tile, FROWS, coefs, 1.0)


def laid(i, rows, outside, state_ref):
    lo8 = low(8)
    zero8 = jnp.zeros((8, W), F32)
    before = jnp.where(lo8, zero8, swap(rows[HALF - 8 :]))
    after = jnp.where(lo8, swap(rows[:8]), zero8)
    if outside is not None:
        rows = jnp.where(outside, jnp.zeros_like(rows), rows)
        before = jnp.where(outside, zero8, before)
        after = jnp.where(outside, zero8, after)
    start = i * FROWS
    state_ref[start : start + 4, :] = zero8[:4]
    state_ref[start + 4 : start + 12, :] = before
    state_ref[start + 12 : start + 76, :] = rows
    state_ref[start + 76 : start + 84, :] = after
    state_ref[start + 84 : start + 88, :] = zero8[:4]


def coarsened(j, state_ref, coarse_ref, sum_ref):
    base = 4 * j * FROWS
    sum_ref[...] = (state_ref[base : base + FROWS, :] + state_ref[base + FROWS : base + 2 * FROWS, :]) + (
        state_ref[base + 2 * FROWS : base + 3 * FROWS, :] + state_ref[base + 3 * FROWS : base + 4 * FROWS, :]
    )
    start = (j + 1) * CROWS
    coarse_ref[start + 7 : start + 27, :] = coarse_rows(sum_ref, 4, 20)


def block_kernel(edge_ref, middle_ref, s0_ref, coarse_ref, sum_ref):
    for i in range(4, 36):
        source, base = block_row(i - 4, edge_ref, middle_ref, None, None)
        laid(i, source[base : base + HALF, :], None, s0_ref)
    coarse_ref[...] = jnp.zeros_like(coarse_ref)
    for j in range(1, 9):
        coarsened(j, s0_ref, coarse_ref, sum_ref)


def inner_kernel(
    west_ref, east_ref, diffuse_ref, wind_ref, s0_in, coarse_in,
    s0_ref, s1_ref, s2_ref, s3_ref, end_ref, coarse_ref, sum_ref,
):
    del s0_in, coarse_in
    for i in (*range(4), *range(36, 40)):
        source, base = block_row(i - 4, None, None, west_ref, east_ref)
        laid(i, source[base : base + HALF, :], lax.axis_index("gx") == (0 if i < 4 else 7), s0_ref)
    coarsened(0, s0_ref, coarse_ref, sum_ref)
    coarsened(9, s0_ref, coarse_ref, sum_ref)
    states = (s0_ref, s1_ref, s2_ref, s3_ref)
    substeps(states, end_ref, coefficients(diffuse_ref, wind_ref), range(9), range(8))


def outer_kernel(
    west_ref, east_ref, left_ref, right_ref, diffuse_ref, wind_ref,
    s0_in, s1_in, s2_in, s3_in, end_in, coarse_in,
    s0_ref, s1_ref, s2_ref, s3_ref, end_ref, coarse_ref, change_ref, send_ref,
    sum_ref, blend_ref, part_ref,
):
    del s0_in, s1_in, s2_in, s3_in, end_in, coarse_in
    first_segment = lax.axis_index("tm") == 0
    at_west = lax.axis_index("gx") == 0
    at_east = lax.axis_index("gx") == 7
    at_left = lax.axis_index("gy") == 0
    at_right = lax.axis_index("gy") == 3
    lo8 = low(8)
    zero8 = jnp.zeros((8, W), F32)
    coefs = coefficients(diffuse_ref, wind_ref)

    for j in range(10):
        befores = []
        afters = []
        for i in range(4 * j, 4 * j + 4):
            k = i % 20
            from_left = left_ref[8 * k : 8 * k + 8, :]
            from_right = right_ref[8 * k : 8 * k + 8, :]
            if i >= 20:
                from_left = swap(from_left)
            else:
                from_right = swap(from_right)
            start = i * FROWS
            known = s0_ref[start + 4 : start + 12, :]
            before = jnp.where(lo8, jnp.where(at_left, zero8, from_left), known)
            known = s0_ref[start + 76 : start + 84, :]
            after = jnp.where(lo8, known, jnp.where(at_right, zero8, from_right))
            if i < 4 or i >= 36:
                outside = at_west if i < 4 else at_east
                before = jnp.where(outside, zero8, before)
                after = jnp.where(outside, zero8, after)
            s0_ref[start + 4 : start + 12, :] = before
            s0_ref[start + 76 : start + 84, :] = after
            befores.append(before)
            afters.append(after)
        base = 16 * j
        sum_ref[base : base + 8, :] = (befores[0] + befores[1]) + (befores[2] + befores[3])
        sum_ref[base + 8 : base + 16, :] = (afters[0] + afters[1]) + (afters[2] + afters[3])
        start = (j + 1) * CROWS
        coarse_ref[start + 7 : start + 9, :] = coarse_rows(sum_ref, base, 2)
        coarse_ref[start + 25 : start + 27, :] = coarse_rows(sum_ref, base + 8, 2)
    left_corner = left_ref[160:168, :]
    right_corner = right_ref[160:168, :]
    for source, start, outside, is_west in (
        (west_ref, 0, at_west, True),
        (east_ref, 11 * CROWS, at_east, False),
    ):
        rows = source[4 * HALF :, :]
        from_left = left_corner if is_west else swap(left_corner)
        from_right = swap(right_corner) if is_west else right_corner
        from_left = jnp.where(at_left, zero8, from_left)
        from_right = jnp.where(at_right, zero8, from_right)
        before = jnp.where(lo8, from_left, swap(rows[8:]))
        after = jnp.where(lo8, swap(rows[:8]), from_right)
        coarse_ref[start + 1 : start + 9, :] = jnp.where(outside, zero8, before)
        coarse_ref[start + 9 : start + 25, :] = jnp.where(outside, jnp.zeros_like(rows), rows)
        coarse_ref[start + 25 : start + 33, :] = jnp.where(outside, zero8, after)

    for j in range(10):
        for tile in range(3):
            image = advanced(coarse_ref, (j + 1) * CROWS + 8 + 8 * tile, CROWS, coefs, 0.25)
            cy = rows_of(8) + (8 * tile - 1)
            outside = cy > CY
            if tile == 0:
                outside = jnp.logical_or(outside, jnp.logical_and(at_left, jnp.logical_and(cy < 0, lo8)))
            if tile == 2:
                outside = jnp.logical_or(
                    outside, jnp.logical_and(at_right, jnp.logical_and(cy >= CY, jnp.logical_not(lo8)))
                )
            if j == 0:
                outside = jnp.logical_or(outside, at_west)
            if j == 9:
                outside = jnp.logical_or(outside, at_east)
            image = jnp.where(outside, zero8, image)
            o = j * OROWS + 8 * tile
            change_ref[o : o + 8, :] = jnp.where(first_segment, image, zero8) - image

    states = (s0_ref, s1_ref, s2_ref, s3_ref)
    substeps(states, end_ref, coefs, (0, 8), (0, 7))

    for j in range(CX):
        lower = change_ref[j * OROWS : (j + 1) * OROWS, :]
        middle = change_ref[(j + 1) * OROWS : (j + 2) * OROWS, :]
        upper = change_ref[(j + 2) * OROWS : (j + 3) * OROWS, :]
        slot = j * OROWS
        blend_ref[slot : slot + OROWS, :] = BLEND[0] * lower + BLEND[1] * middle + BLEND[2] * upper
        blended = (
            BLEND[0] * blend_ref[slot : slot + CY, :]
            + BLEND[1] * blend_ref[slot + 1 : slot + CY + 1, :]
            + BLEND[2] * blend_ref[slot + 2 : slot + CY + 2, :]
        )
        base = 4 * j * HALF
        total = (end_ref[base : base + HALF, :] + end_ref[base + HALF : base + 2 * HALF, :]) + (
            end_ref[base + 2 * HALF : base + 3 * HALF, :] + end_ref[base + 3 * HALF : base + 4 * HALF, :]
        )
        spot = 160 + j * HALF
        sum_ref[spot : spot + HALF, :] = total
        part_ref[j * CY : (j + 1) * CY, :] = coarse_rows(sum_ref, spot, CY) + blended
    turned = part_ref[...].T
    for h in range(2):
        send_ref[pl.ds(h, LEVELS, stride=2), :] = turned[h * LEVELS : (h + 1) * LEVELS]


def split_kernel(part_ref, first_ref, second_ref):
    first_ref[...] = part_ref[pl.ds(0, LEVELS, stride=2), :]
    second_ref[...] = part_ref[pl.ds(1, LEVELS, stride=2), :]


def chain_kernel(level_ref, part_ref, left_ref, right_ref, send_ref):
    at_left = lax.axis_index("gy") == 0
    at_right = lax.axis_index("gy") == 3
    spread = (0.25 * STEP) * level_ref[0:8, :]
    along_x = (0.5 * STEP) * level_ref[8:16, :]
    along_y = (0.5 * STEP) * level_ref[16:24, :]

    lane = lanes(8)
    row = rows_of(8)
    column = lane % 16
    zero = jnp.zeros((8, W), F32)

    def neighbours(tile):
        up = jnp.where(row < 7, pltpu.roll(tile, 7, 0), zero)
        down = jnp.where(row > 0, pltpu.roll(tile, 1, 0), zero)
        return up, down

    def along_rows(tile, up, down):
        east = pltpu.roll(jnp.where(lane < 16, up, tile), W - 16, 1)
        west = pltpu.roll(jnp.where(lane >= W - 16, down, tile), 16, 1)
        return east, west

    def along_columns(tiles):
        after = [pltpu.roll(tile, W - 1, 1) for tile in tiles]
        before = [pltpu.roll(tile, 1, 1) for tile in tiles]
        after_far = [pltpu.roll(tile, 15, 1) for tile in tiles[1:]] + [zero]
        before_far = [zero] + [pltpu.roll(tile, W - 15, 1) for tile in tiles[:-1]]
        north = [jnp.where(column < 15, near, far) for near, far in zip(after, after_far)]
        south = [jnp.where(column > 0, near, far) for near, far in zip(before, before_far)]
        return north, south

    def cleared(tiles):
        return [jnp.where(at_left, zero, tiles[0]), tiles[1], tiles[2], jnp.where(at_right, zero, tiles[3])]

    def part(n):
        return cleared(
            [
                left_ref[8 * n : 8 * n + 8, :],
                part_ref[pl.ds(16 * n, 8, stride=2), :],
                part_ref[pl.ds(16 * n + 1, 8, stride=2), :],
                right_ref[8 * n : 8 * n + 8, :],
            ]
        )

    item = lane % 64
    end_lane = jnp.where(item < 16, item + (W - 16), jnp.where(item < 32, item - 16, 0))
    side_lane = jnp.clip(jnp.where(item < 48, (item - 33) * 16 + 15, (item - 49) * 16), 0, W - 1)
    corner_lane = jnp.where(item < 40, W - 1, jnp.where(item < 45, 15, jnp.where(item < 52, W - 16, 0)))
    is_corner = (item == 32) | (item == 41) | (item == 48) | (item == 57)

    def picked(values, index):
        return jnp.take_along_axis(values, index, axis=1)

    for r in range(3):
        send_ref[pl.ds(r, 8, stride=3), :] = zero
    coarse = part(0)
    for n in range(1, 8):
        north, south = along_columns(coarse)
        image = []
        for b in range(4):
            east, west = along_rows(coarse[b], *neighbours(coarse[b]))
            slope = along_x * (east - west) + along_y * (north[b] - south[b])
            total = (east + west) + (north[b] + south[b])
            image.append(coarse[b] + (spread * (total - 4.0 * coarse[b]) - coarse[b] * slope))
        image = cleared(image)
        beside = [neighbours(tile) for tile in image]

        rows = []
        for b in (1, 2):
            ends = picked(jnp.where(lane >= 64, beside[b][1], beside[b][0]), end_lane)
            sides = picked(jnp.where(column == 15, image[b - 1], image[b + 1]), side_lane)
            corners = jnp.where(
                lane >= 64,
                jnp.where(column == 15, beside[b - 1][1], beside[b + 1][1]),
                jnp.where(column == 15, beside[b - 1][0], beside[b + 1][0]),
            )
            corners = picked(corners, corner_lane)
            rows.append(jnp.where(item < 32, ends, jnp.where(is_corner, corners, sides)))
        base = n * 24
        send_ref[pl.ds(base, 8, stride=3), :] = image[1]
        send_ref[pl.ds(base + 1, 8, stride=3), :] = image[2]
        send_ref[pl.ds(base + 2, 8, stride=3), :] = jnp.where(lane < 64, rows[0], rows[1])

        if n < 7:
            blended = []
            for tile, pair in zip(image, beside):
                east, west = along_rows(tile, *pair)
                blended.append(BLEND[0] * west + BLEND[1] * tile + BLEND[2] * east)
            north, south = along_columns(blended)
            coarse = cleared(
                [
                    value + (BLEND[0] * s + BLEND[1] * tile + BLEND[2] * n_)
                    for value, s, tile, n_ in zip(part(n), south, blended, north)
                ]
            )


def base_kernel(end_ref, change_ref, base_ref, along_ref, fine_ref):
    lo = low(HALF)
    for j in range(CX):
        lower = change_ref[j * OROWS : (j + 1) * OROWS, :]
        middle = change_ref[(j + 1) * OROWS : (j + 2) * OROWS, :]
        upper = change_ref[(j + 2) * OROWS : (j + 3) * OROWS, :]
        for offset in range(4):
            along = WEIGHTS_MID[offset] * middle
            if offset < 2:
                along = along + WEIGHTS_LOW[offset] * lower
            else:
                along = along + WEIGHTS_HIGH[offset] * upper
            slot = offset * OROWS
            along_ref[slot : slot + OROWS, :] = along
            before = along_ref[slot : slot + CY, :]
            centre = along_ref[slot + 1 : slot + CY + 1, :]
            after = along_ref[slot + 2 : slot + CY + 2, :]
            for k in range(4):
                value = WEIGHTS_MID[k] * centre
                if k < 2:
                    value = value + WEIGHTS_LOW[k] * before
                else:
                    value = value + WEIGHTS_HIGH[k] * after
                fine_ref[pl.ds(offset * HALF + k, CY, stride=4), :] = value
        for pair in range(2):
            x = 4 * j + 2 * pair
            one = end_ref[x * HALF : (x + 1) * HALF, :] + fine_ref[2 * pair * HALF : (2 * pair + 1) * HALF, :]
            two = (
                end_ref[(x + 1) * HALF : (x + 2) * HALF, :]
                + fine_ref[(2 * pair + 1) * HALF : (2 * pair + 2) * HALF, :]
            )
            both = jnp.concatenate([jnp.where(lo, one, swap(two)), jnp.where(lo, swap(one), two)], axis=0).T
            base_ref[x * LEVELS : (x + 2) * LEVELS, :] = both


def column_weights():
    weights = np.zeros((3 * W, 10, W), np.float32)

    def put(k, j, cy):
        for offset in range(4):
            for at, factor in ((4 * (cy + 1), WEIGHTS_LOW), (4 * cy, WEIGHTS_MID), (4 * (cy - 1), WEIGHTS_HIGH)):
                if 0 <= at + offset < W:
                    weights[k, j, at + offset] += factor[offset]

    for h in range(2):
        for cx in range(CX):
            for c in range(CY):
                put(h * W + cx * CY + c, cx + 1, h * CY + c)
        for c in range(CY):
            put(2 * W + h * 64 + c, 0, h * CY + c)
            put(2 * W + h * 64 + CY + c, 9, h * CY + c)
        for j in range(10):
            if h == 0:
                put(2 * W + 32 + j, j, -1)
            else:
                put(2 * W + 64 + 48 + j, j, 2 * CY)
    return weights.reshape(3 * W, 10 * W).astype(ml_dtypes.bfloat16)


def end_kernel(base_ref, back_ref, weights_ref, out_ref, stage_ref, sem):
    values = jnp.concatenate([back_ref[pl.ds(r, LEVELS, stride=3), :] for r in range(3)], axis=1)
    first = values.astype(jnp.bfloat16)
    rest = values - first.astype(F32)
    second = rest.astype(jnp.bfloat16)
    third = (rest - second.astype(F32)).astype(jnp.bfloat16)
    stacked = jnp.concatenate([first, second, third], axis=0)
    columns = []
    copies = []
    for pair in range(5):
        product = jnp.dot(
            stacked, weights_ref[:, 2 * pair * W : 2 * (pair + 1) * W], preferred_element_type=F32
        )
        product = product[:LEVELS] + (product[LEVELS : 2 * LEVELS] + product[2 * LEVELS :])
        columns += [product[:, :W], product[:, W:]]
        if pair == 0:
            continue
        block = pair - 1
        for j in range(2 * block, 2 * block + 2):
            for offset in range(4):
                value = WEIGHTS_MID[offset] * columns[j + 1]
                if offset < 2:
                    value = value + WEIGHTS_LOW[offset] * columns[j]
                else:
                    value = value + WEIGHTS_HIGH[offset] * columns[j + 2]
                x = 4 * j + offset
                stage_ref[pl.ds(block * 8 * LEVELS + x % 8, LEVELS, stride=8), :] = (
                    base_ref[x * LEVELS : (x + 1) * LEVELS, :] + value
                )
        copy = pltpu.make_async_copy(
            stage_ref.reshape(4, LEVELS, 8, W).at[block], out_ref.at[:, pl.ds(8 * block, 8), :], sem.at[block]
        )
        copy.start()
        copies.append(copy)
    for copy in copies:
        copy.wait()


def shape(rows):
    return jax.ShapeDtypeStruct((rows, W), F32)


VMEM = pl.BlockSpec(memory_space=pltpu.VMEM)
HBM = pl.BlockSpec(memory_space=pltpu.HBM)


def scratch(rows):
    return pltpu.VMEM((rows, W), F32)


def call(kernel, out_shape, in_specs, scratch_shapes, name, aliases=None, out_specs=None, cost=None, limit=24):
    many = isinstance(out_shape, tuple)
    return pl.pallas_call(
        kernel,
        out_shape=out_shape,
        in_specs=in_specs,
        out_specs=out_specs or ((VMEM,) * len(out_shape) if many else VMEM),
        scratch_shapes=scratch_shapes,
        input_output_aliases=aliases or {},
        cost_estimate=cost,
        compiler_params=pltpu.CompilerParams(vmem_limit_bytes=limit * 1024 * 1024),
        name=name,
    )


def ring(array, axis, distance):
    devices = lax.axis_size(axis)
    return lax.ppermute(array, axis, [(i, (i + distance) % devices) for i in range(devices)])


def shards(state_starts, diffusivity, wind):
    field = state_starts.reshape(LEVELS, NX, W)
    edges, first_rows, last_rows = call(
        edge_kernel,
        (shape(16 * HALF), shape(STRIP), shape(STRIP)),
        [VMEM] * 2,
        [scratch(HALF)],
        "edges",
    )(field[:, :8].reshape(8 * LEVELS, W), field[:, NX - 8 :].reshape(8 * LEVELS, W))
    west = ring(last_rows, "gx", 1)
    east = ring(first_rows, "gx", -1)
    middle = call(
        middle_kernel,
        shape(16 * HALF),
        [VMEM],
        [],
        "middle",
        cost=pl.CostEstimate(flops=1 << 20, bytes_accessed=1 << 20, transcendentals=0),
    )(field[:, 8 : NX - 8].reshape(16 * LEVELS, W))
    block, coarse = call(
        block_kernel,
        (shape(40 * FROWS), shape(12 * CROWS)),
        [VMEM] * 2,
        [scratch(FROWS)],
        "block",
        cost=pl.CostEstimate(flops=1 << 20, bytes_accessed=1 << 20, transcendentals=0),
    )(edges, middle)
    first_columns, last_columns = call(side_kernel, (shape(SIDE), shape(SIDE)), [VMEM] * 4, [], "sides")(
        edges, middle, west, east
    )
    first_columns, last_columns, block, coarse = lax.optimization_barrier(
        (first_columns, last_columns, block, coarse)
    )
    left = ring(last_columns, "gy", 1)
    right = ring(first_columns, "gy", -1)
    level = lax.axis_index("tm") * 8 + lax.axis_index("gx")
    of_level = jnp.concatenate([diffusivity[None], wind], axis=0)
    of_level = lax.dynamic_slice_in_dim(of_level, level, 1, axis=1)
    of_level = jnp.broadcast_to(of_level[:, None, :], (3, 8, W)).reshape(24, W)
    diffuse_row = diffusivity.reshape(1, LEVELS)
    states = (shape(40 * FROWS),) * 4 + (shape(NX * HALF), shape(12 * CROWS))
    inner = call(
        inner_kernel,
        states,
        [VMEM] * 6,
        [scratch(FROWS)],
        "inner",
        aliases={4: 0, 5: 5},
        cost=pl.CostEstimate(flops=1 << 24, bytes_accessed=8 << 20, transcendentals=0),
    )(west, east, diffuse_row, wind, block, coarse)
    outer = call(
        outer_kernel,
        states + (shape(10 * OROWS), shape(2 * LEVELS)),
        [VMEM] * 12,
        [scratch(160 + CX * HALF), scratch(CX * OROWS), scratch(W)],
        "outer",
        aliases={6 + k: k for k in range(6)},
    )(west, east, left, right, diffuse_row, wind, *inner)
    fine_end, change, parts = outer[4], outer[6], outer[7]
    parts = lax.all_to_all(parts.reshape(LEVELS, 2, W), ("tm", "gx"), 0, 0, tiled=True).reshape(2 * LEVELS, W)
    first_half, second_half = call(split_kernel, (shape(LEVELS), shape(LEVELS)), [VMEM], [], "split")(parts)
    left = ring(second_half, "gy", 1)
    right = ring(first_half, "gy", -1)
    parts, fine_end = lax.optimization_barrier((parts, fine_end))
    base = call(
        base_kernel,
        shape(NX * LEVELS),
        [VMEM] * 2,
        [scratch(4 * OROWS), scratch(4 * HALF)],
        "base",
        cost=pl.CostEstimate(flops=1 << 22, bytes_accessed=2 << 20, transcendentals=0),
    )(fine_end, change)
    left, right, base = lax.optimization_barrier((left, right, base))
    images = call(chain_kernel, shape(3 * LEVELS), [VMEM] * 4, [], "chain")(
        of_level, parts, left, right
    )
    images = lax.all_to_all(images.reshape(LEVELS, 1, 3 * W), ("tm", "gx"), 0, 0, tiled=True)
    ending = call(
        end_kernel,
        jax.ShapeDtypeStruct((LEVELS, NX, W), F32),
        [VMEM] * 3,
        [scratch(NX * LEVELS), pltpu.SemaphoreType.DMA((4,))],
        "ending",
        out_specs=HBM,
    )(base, images.reshape(3 * LEVELS, W), jnp.asarray(column_weights()))
    return ending.reshape(1, LEVELS, NX, W)


def solution(mesh):
    placed = (P("tm", None, "gx", "gy"), P(), P())
    return jax.shard_map(
        shards, mesh=mesh, in_specs=placed, out_specs=P("tm", None, "gx", "gy"), check_vma=False
    )
```
